256 devices in a mesh: batch: 64 (over y, x, z_hi), chan: 4 (over z_lo, core).
Axes of the slice: x: 4, y: 4, z: 8 (z_hi: 4, z_lo: 2; z = z_hi * 2 + z_lo), core: 2. Of those that a mesh axis runs over, the one named last changes fastest.
Arguments:
- fine_inputs: bfloat16 [64, 32, 32, 512], P('batch'), may hold values from -6 to 6
- fine_upstream: bfloat16 [64, 32, 32, 512], P('batch', None, None, 'chan'), may hold values from -6 to 6
- fine_bank: bfloat16 [8, 9, 512, 512], P(None, None, 'batch', 'chan'), may hold values from -0.09375 to 0.09375
- fine_coefs: float32 [64, 8], replicated, may hold values from 0 to 1, as said below
- coarse_inputs: bfloat16 [64, 16, 16, 512], P('batch'), may hold values from -6 to 6
- coarse_upstream: bfloat16 [64, 16, 16, 512], P('batch', None, None, 'chan'), may hold values from -6 to 6
- coarse_bank: bfloat16 [8, 9, 512, 512], P(None, None, 'batch', 'chan'), may hold values from -0.09375 to 0.09375
- coarse_coefs: float32 [64, 8], replicated, may hold values from 0 to 1, as said below
Outputs:
- fine_delta: bfloat16 [64, 32, 32, 512], P('batch', None, None, 'chan')
- fine_update: float32 [8, 9, 512, 512], P(None, None, 'batch', 'chan')
- fine_logit: float32 [64, 8], P('batch')
- coarse_delta: bfloat16 [64, 16, 16, 512], P('batch', None, None, 'chan')
- coarse_update: float32 [8, 9, 512, 512], P(None, None, 'batch', 'chan')
- coarse_logit: float32 [64, 8], P('batch')
The draws below stay inside these ranges and needn't reach their ends.
Inputs may be any that keep to these rules, and one draw needn't show every extreme that they name: Each row of fine_coefs is a softmax: positive entries that sum to one. Each row of coarse_coefs is a softmax: positive entries that sum to one.
All inputs are finite; a program needn't handle non-finite values.
Results may differ from the reference program's by a relative error of at most 0.01.
Values may be sent and summed in bfloat16 or wider, within the bound.
A program may use at most 128 MiB of HBM per device.

```python
import jax
import jax.numpy as jnp
from jax import lax

CHANNELS_IN = 512
CHANNELS_OUT = 512
BANKS = 8
FINE_SIDE = 32
COARSE_SIDE = 16
SAMPLES = 64
N_CHAN = 4


def softmax_rows(key, salt):
    sub = jax.random.fold_in(key, salt)
    logits = 1.5 * jax.random.normal(sub, (SAMPLES, BANKS), jnp.float32)
    return jax.nn.softmax(logits, axis=1).astype(jnp.float32)


def draw_fine_coefs(key, part):
    return softmax_rows(key, 11)


def draw_coarse_coefs(key, part):
    return softmax_rows(key, 23)


def block_levels(rng, shape, split, low, largest):
    factor_of, own = 1.0, jax.random.fold_in(rng, 6)
    for axis_at, parts in split:
        heights = jnp.exp(jax.random.uniform(jax.random.fold_in(own, axis_at), (parts,), jnp.float32, low / len(split), largest / len(split)))
        factor_of = factor_of * jnp.repeat(heights, shape[axis_at] // parts).reshape([-1 if axis == axis_at else 1 for axis in range(len(shape))])
    return factor_of


def bell_draw(stream_key, shape, spread, limit, cuts=(), kind=jnp.bfloat16):
    result = jax.random.normal(stream_key, shape, jnp.float32) * spread
    if len(cuts) > 0:
        result = block_levels(stream_key, shape, cuts, -0.22, 0.18) * result
    return jnp.clip(result, min=-limit, max=limit).astype(kind)


def setup_inputs(seed: int = 0) -> dict:
    streams_of = jax.random.split(jax.random.key(seed), 9)
    return {
        "fine_inputs": bell_draw(streams_of[0], (SAMPLES, FINE_SIDE, FINE_SIDE, CHANNELS_IN), 1.0, 6.0, ((0, 64),)),
        "fine_upstream": bell_draw(streams_of[1], (SAMPLES, FINE_SIDE, FINE_SIDE, CHANNELS_OUT), 1.0, 6.0, ((0, 64), (3, 4))),
        "fine_bank": bell_draw(streams_of[2], (BANKS, 9, CHANNELS_IN, CHANNELS_OUT), (9 * CHANNELS_IN) ** -0.5, 0.09375, ((2, 64), (3, 4))),
        "fine_coefs": draw_fine_coefs(jax.random.fold_in(streams_of[8], 71), 0),
        "coarse_inputs": bell_draw(streams_of[4], (SAMPLES, COARSE_SIDE, COARSE_SIDE, CHANNELS_IN), 1.0, 6.0, ((0, 64),)),
        "coarse_upstream": bell_draw(streams_of[5], (SAMPLES, COARSE_SIDE, COARSE_SIDE, CHANNELS_OUT), 1.0, 6.0, ((0, 64), (3, 4))),
        "coarse_bank": bell_draw(streams_of[6], (BANKS, 9, CHANNELS_IN, CHANNELS_OUT), (9 * CHANNELS_IN) ** -0.5, 0.09375, ((2, 64), (3, 4))),
        "coarse_coefs": draw_coarse_coefs(jax.random.fold_in(streams_of[8], 71), 0),
    }


HIGH = lax.Precision.HIGHEST


def mix_kernels(coefs, bank_all):
    flat = bank_all.reshape(bank_all.shape[0], -1).astype(jnp.float32)
    mixed = jnp.dot(coefs, flat, precision=HIGH)
    return mixed.reshape((coefs.shape[0],) + bank_all.shape[1:]).astype(jnp.bfloat16)


def sample_backward(inputs, upstream, kernel, side):
    padded_in = jnp.pad(inputs, ((1, 1), (1, 1), (0, 0))).astype(jnp.float32)
    padded_up = jnp.pad(upstream, ((1, 1), (1, 1), (0, 0))).astype(jnp.float32)
    flat_up = upstream.astype(jnp.float32).reshape(side * side, -1)
    kernel_f = kernel.astype(jnp.float32)
    group = CHANNELS_OUT // N_CHAN
    grad_taps = []
    windows_up = []
    for row_shift in range(3):
        for col_shift in range(3):
            window_in = padded_in[row_shift:row_shift + side, col_shift:col_shift + side, :].reshape(side * side, -1)
            grad_taps.append(jnp.dot(window_in.T, flat_up, precision=HIGH) / side)
            windows_up.append(padded_up[2 - row_shift:2 - row_shift + side, 2 - col_shift:2 - col_shift + side, :].reshape(side * side, -1))
    delta = jnp.zeros((side * side, CHANNELS_IN), jnp.float32)
    for which in range(N_CHAN):
        partial_sum = jnp.zeros((side * side, CHANNELS_IN), jnp.float32)
        for tap in range(9):
            cols = windows_up[tap][:, which * group:(which + 1) * group]
            weights = kernel_f[tap][:, which * group:(which + 1) * group]
            partial_sum = partial_sum + jnp.dot(cols, weights.T, precision=HIGH)
        delta = delta + partial_sum.astype(jnp.bfloat16).astype(jnp.float32)
    return delta.astype(jnp.bfloat16).reshape(side, side, CHANNELS_IN), jnp.stack(grad_taps, axis=0)


def layer_backward(inputs, upstream, bank_all, coefs, side):
    kernels = mix_kernels(coefs, bank_all)
    flat_bank = bank_all.reshape(BANKS, -1).astype(jnp.float32)

    def step(total, items):
        x_in, g_up, kern, coef_row = items
        delta, grad = sample_backward(x_in, g_up, kern, side)
        flat_grad = grad.reshape(-1)
        dcoef = jnp.dot(flat_bank, flat_grad, precision=HIGH)
        total = total + coef_row[:, None] * flat_grad[None, :]
        return total, (delta, dcoef)

    start = jnp.zeros((BANKS, 9 * CHANNELS_IN * CHANNELS_OUT), jnp.float32)
    total, (deltas, dcoefs) = lax.scan(step, start, (inputs, upstream, kernels, coefs))
    logit = coefs * (dcoefs - jnp.sum(coefs * dcoefs, axis=1, keepdims=True))
    return deltas, total.reshape(bank_all.shape), logit


def reference(fine_inputs, fine_upstream, fine_bank, fine_coefs, coarse_inputs, coarse_upstream, coarse_bank, coarse_coefs):
    fine_delta, fine_update, fine_logit = layer_backward(fine_inputs, fine_upstream, fine_bank, fine_coefs, FINE_SIDE)
    coarse_delta, coarse_update, coarse_logit = layer_backward(coarse_inputs, coarse_upstream, coarse_bank, coarse_coefs, COARSE_SIDE)
    return (fine_delta, fine_update, fine_logit, coarse_delta, coarse_update, coarse_logit)
```

```python
import functools

import jax
import jax.numpy as jnp
from jax import lax
from jax.experimental import pallas as pl
from jax.experimental.pallas import tpu as pltpu
from jax.sharding import PartitionSpec as P

BANKS = 8
TAPS = 9
CHANNELS = 512
GROUP = 128
FINE_SIDE = 32
COARSE_SIDE = 16
N_XY = 16
N_Z = 4
N_CHAN = 4
ROWS = CHANNELS // N_XY
OWN = 8
WIDE = TAPS * GROUP
ROW3 = 3 * GROUP

MESH = pl.DeviceIdType.MESH
HIGH = lax.Precision.HIGHEST
F32 = jnp.float32
BF16 = jnp.bfloat16


def iota(shape, axis):
    return lax.broadcasted_iota(jnp.int32, shape, axis)


def mm(a, b, contract, precision=None):
    dims = (((contract[0],), (contract[1],)), ((), ()))
    return lax.dot_general(a, b, dims, precision=precision, preferred_element_type=F32)


class Layer:
    def __init__(self, side, inputs, upstream, bank, coefs, delta, update, logit, scratch):
        self.side = side
        self.inputs, self.upstream, self.bank, self.coefs = inputs, upstream, bank, coefs
        self.delta, self.update, self.logit = delta, update, logit
        (
            self.shifts, self.banks, self.mix_hi, self.mix_lo, self.back_hi, self.back_lo,
            self.grad_out, self.grad_in, self.kern_out, self.kern_in,
            self.part, self.part_out, self.part_in, self.diff, self.diff_out, self.diff_in,
            self.bank_ss, self.bank_rs, self.grad_ss, self.grad_rs, self.kern_ss, self.kern_rs,
            self.part_ss, self.part_rs, self.diff_ss, self.diff_rs,
        ) = scratch


def layer_scratch(side):
    pixels = side * side
    return [
        pltpu.VMEM((pixels + 2 * side, ROW3), BF16),
        pltpu.VMEM((N_Z * BANKS * OWN, WIDE), BF16),
        pltpu.VMEM((CHANNELS, N_Z * BANKS * OWN), BF16),
        pltpu.VMEM((CHANNELS, N_Z * BANKS * OWN), BF16),
        pltpu.VMEM((N_Z * BANKS * OWN, CHANNELS), BF16),
        pltpu.VMEM((N_Z * BANKS * OWN, CHANNELS), BF16),
        pltpu.VMEM((CHANNELS, WIDE), BF16),
        pltpu.VMEM((CHANNELS, WIDE), BF16),
        pltpu.VMEM((CHANNELS, WIDE), BF16),
        pltpu.VMEM((CHANNELS, WIDE), BF16),
        pltpu.VMEM((BANKS * OWN, WIDE), F32),
        pltpu.VMEM((N_Z, BANKS * OWN, WIDE), BF16),
        pltpu.VMEM((N_Z, BANKS * OWN, WIDE), BF16),
        pltpu.VMEM((pixels, GROUP), F32),
        pltpu.VMEM((N_CHAN, pixels, GROUP), BF16),
        pltpu.VMEM((N_CHAN, pixels, GROUP), BF16),
    ] + [
        pltpu.SemaphoreType.DMA((n,))
        for n in (N_Z, N_Z, N_XY, N_XY, N_XY, N_XY, N_Z, N_Z, N_CHAN, N_CHAN)
    ]


N_LAYER_SCRATCH = 26


class Place:
    def __init__(self):
        self.batch = lax.axis_index("batch")
        self.chan = lax.axis_index("chan")
        self.xy = self.batch // N_Z
        self.z = self.batch % N_Z

    def at_xy(self, xy):
        return (xy * N_Z + self.z, self.chan)

    def at_z(self, z):
        return (self.xy * N_Z + z, self.chan)

    def at_chan(self, chan):
        return (self.batch, chan)


def rows_of(index, count):
    return pl.ds(pl.multiple_of(index * count, count), count)


def bank_copy(layer, place, z_to, z_from):
    return pltpu.make_async_remote_copy(
        src_ref=layer.banks.at[rows_of(z_from, BANKS * OWN)],
        dst_ref=layer.banks.at[rows_of(z_from, BANKS * OWN)],
        send_sem=layer.bank_ss.at[z_to],
        recv_sem=layer.bank_rs.at[z_from],
        device_id=place.at_z(z_to),
        device_id_type=MESH,
    )


def grad_copy(layer, place, xy_to, xy_from):
    return pltpu.make_async_remote_copy(
        src_ref=layer.grad_out.at[rows_of(xy_to, ROWS)],
        dst_ref=layer.grad_in.at[rows_of(xy_from, ROWS)],
        send_sem=layer.grad_ss.at[xy_to],
        recv_sem=layer.grad_rs.at[xy_from],
        device_id=place.at_xy(xy_to),
        device_id_type=MESH,
    )


def kern_copy(layer, place, xy_to, xy_from):
    return pltpu.make_async_remote_copy(
        src_ref=layer.kern_out.at[rows_of(xy_to, ROWS)],
        dst_ref=layer.kern_in.at[rows_of(xy_from, ROWS)],
        send_sem=layer.kern_ss.at[xy_to],
        recv_sem=layer.kern_rs.at[xy_from],
        device_id=place.at_xy(xy_to),
        device_id_type=MESH,
    )


def part_copy(layer, place, z_to, z_from):
    return pltpu.make_async_remote_copy(
        src_ref=layer.part_out.at[z_to],
        dst_ref=layer.part_in.at[z_from],
        send_sem=layer.part_ss.at[z_to],
        recv_sem=layer.part_rs.at[z_from],
        device_id=place.at_z(z_to),
        device_id_type=MESH,
    )


def diff_copy(layer, place, chan_to, chan_from):
    return pltpu.make_async_remote_copy(
        src_ref=layer.diff_out.at[chan_to],
        dst_ref=layer.diff_in.at[chan_from],
        send_sem=layer.diff_ss.at[chan_to],
        recv_sem=layer.diff_rs.at[chan_from],
        device_id=place.at_chan(chan_to),
        device_id_type=MESH,
    )


def coef_copy(out_ref, in_ref, send_sem, recv_sem, place, xy_to, xy_from):
    return pltpu.make_async_remote_copy(
        src_ref=out_ref.at[xy_to],
        dst_ref=in_ref.at[xy_from],
        send_sem=send_sem.at[xy_to],
        recv_sem=recv_sem.at[xy_from],
        device_id=place.at_xy(xy_to),
        device_id_type=MESH,
    )


def total_copy(ref, send_sem, recv_sem, place, chan_to, chan_from):
    return pltpu.make_async_remote_copy(
        src_ref=ref.at[chan_from],
        dst_ref=ref.at[chan_from],
        send_sem=send_sem.at[chan_to],
        recv_sem=recv_sem.at[chan_from],
        device_id=place.at_chan(chan_to),
        device_id_type=MESH,
    )


def loop(low, high, body):
    lax.fori_loop(low, high, lambda n, carry: (body(n), carry)[1], 0)


def arrange_bank(layer, place):
    for tap in range(TAPS):
        rows = layer.bank[:, tap].astype(F32).reshape(BANKS * OWN, GROUP).astype(BF16)
        layer.banks[rows_of(place.z, BANKS * OWN), tap * GROUP : (tap + 1) * GROUP] = rows


def shift_upstream(layer):
    side = layer.side
    pixels = side * side
    up = layer.upstream[...].astype(F32)
    column = iota((pixels, GROUP), 0) % side
    after = jnp.where(column < side - 1, pltpu.roll(up, pixels - 1, 0), 0.0)
    before = jnp.where(column > 0, pltpu.roll(up, 1, 0), 0.0)
    zeros = jnp.zeros((side, ROW3), BF16)
    layer.shifts[0:side] = zeros
    layer.shifts[side + pixels : 2 * side + pixels] = zeros
    for index, value in enumerate((after, up, before)):
        layer.shifts[side : side + pixels, index * GROUP : (index + 1) * GROUP] = value.astype(BF16)


def window(layer, row_shift):
    start = (2 - row_shift) * layer.side
    return layer.shifts[start : start + layer.side * layer.side]


def split(value, hi_ref, lo_ref):
    hi = value.astype(BF16)
    hi_ref[...] = hi
    lo_ref[...] = (value - hi.astype(F32)).astype(BF16)


def spread_coefs(layer, place):
    bank_rows = N_Z * BANKS * OWN
    own = layer.coefs[pl.ds(place.z, N_XY, stride=N_Z), :]
    col = iota((BANKS, bank_rows), 1)
    wide = mm(own, ((col // OWN) % BANKS == iota((BANKS, bank_rows), 0)).astype(F32), (1, 0), HIGH)
    wide = jnp.broadcast_to(wide[:, None, :], (N_XY, ROWS, bank_rows)).reshape(CHANNELS, bank_rows)
    split(jnp.where(diagonal(), wide, 0.0), layer.mix_hi, layer.mix_lo)
    col = iota((N_XY, CHANNELS), 1)
    tall = mm(own, (col // ROWS == iota((N_XY, CHANNELS), 0)).astype(F32), (0, 0), HIGH)
    tall = jnp.broadcast_to(tall[:, None, :], (BANKS, OWN, CHANNELS)).reshape(BANKS * OWN, CHANNELS)
    tall = jnp.broadcast_to(tall[None], (N_Z, BANKS * OWN, CHANNELS)).reshape(bank_rows, CHANNELS)
    row, col = iota((bank_rows, CHANNELS), 0), iota((bank_rows, CHANNELS), 1)
    same = (row // (BANKS * OWN)) * OWN + row % OWN == col % ROWS
    split(jnp.where(same, tall, 0.0), layer.back_hi, layer.back_lo)


def diagonal():
    shape = (CHANNELS, N_Z * BANKS * OWN)
    row, col = iota(shape, 0), iota(shape, 1)
    return row % ROWS == (col // (BANKS * OWN)) * OWN + col % OWN


def send_grads(layer, place):
    my_y = place.xy // 4

    def chunk(n):
        y = (my_y + 1 + n) % 4
        part = pl.ds(pl.multiple_of(y * GROUP, GROUP), GROUP)
        flipped = layer.inputs[:, part].T
        for row_shift in range(3):
            grad = mm(flipped, window(layer, row_shift), (1, 0)) * (1.0 / layer.side)
            layer.grad_out[part, row_shift * ROW3 : (row_shift + 1) * ROW3] = grad.astype(BF16)
        for x in range(4):
            to = y * 4 + (place.xy + 1 + x) % 4

            @pl.when(to != place.xy)
            def _():
                grad_copy(layer, place, to, place.xy).start()

    loop(0, 4, chunk)
    own = rows_of(place.xy, ROWS)
    layer.grad_in[own, :] = layer.grad_out[own, :]


def send_kernels(layer, place):
    my_y = place.xy // 4
    loop(1, N_Z, lambda n: bank_copy(layer, place, place.z, (place.z + n) % N_Z).wait_recv())

    def chunk(n):
        y = (my_y + 1 + n) % 4
        part = pl.ds(pl.multiple_of(y * GROUP, GROUP), GROUP)
        for row_shift in range(3):
            cols = slice(row_shift * ROW3, (row_shift + 1) * ROW3)
            banks = layer.banks[:, cols]
            mixed = mm(layer.mix_hi[part], banks, (1, 0)) + mm(layer.mix_lo[part], banks, (1, 0))
            layer.kern_out[part, cols] = mixed.astype(BF16)
        for x in range(4):
            to = y * 4 + (place.xy + 1 + x) % 4

            @pl.when(to != place.xy)
            def _():
                kern_copy(layer, place, to, place.xy).start()

    loop(0, 4, chunk)
    own = rows_of(place.xy, ROWS)
    layer.kern_in[own, :] = layer.kern_out[own, :]


def send_parts(layer, place):
    loop(1, N_XY, lambda n: grad_copy(layer, place, place.xy, (place.xy + n) % N_XY).wait_recv())

    def chunk(n):
        z = (place.z + 1 + n) % N_Z
        part = rows_of(z, BANKS * OWN)
        for row_shift in range(3):
            cols = slice(row_shift * ROW3, (row_shift + 1) * ROW3)
            grads = layer.grad_in[:, cols]
            total = mm(layer.back_hi[part], grads, (1, 0)) + mm(layer.back_lo[part], grads, (1, 0))
            layer.part[:, cols] = total
            layer.part_out[z, :, cols] = total.astype(BF16)

        @pl.when(z != place.z)
        def _():
            part_copy(layer, place, z, place.z).start()

    loop(0, N_Z, chunk)


def coef_sums(layer):
    bank_rows = N_Z * BANKS * OWN
    cross = mm(layer.grad_in[...], layer.banks[...], (1, 1))
    cross = jnp.where(diagonal(), cross, 0.0).reshape(N_XY, ROWS, bank_rows).sum(axis=1)
    row = iota((bank_rows, GROUP), 0)
    pick = ((row // OWN) % BANKS == iota((bank_rows, GROUP), 1)).astype(F32)
    return mm(cross, pick, (1, 0), HIGH)


def send_diffs(layer, place):
    def chunk(n):
        chan = (place.chan + 1 + n) % N_CHAN
        for x in range(4):
            source = chan * 4 + x

            @pl.when(source != place.xy)
            def _():
                kern_copy(layer, place, place.xy, source).wait_recv()

        part = pl.ds(pl.multiple_of(chan * GROUP, GROUP), GROUP)
        diff = mm(window(layer, 0), layer.kern_in[part, 0:ROW3], (1, 1))
        for row_shift in (1, 2):
            cols = slice(row_shift * ROW3, (row_shift + 1) * ROW3)
            diff = diff + mm(window(layer, row_shift), layer.kern_in[part, cols], (1, 1))
        layer.diff[...] = diff
        layer.diff_out[chan] = diff.astype(BF16)

        @pl.when(chan != place.chan)
        def _():
            diff_copy(layer, place, chan, place.chan).start()

    loop(0, N_CHAN, chunk)


def finish_update(layer, place):
    total = layer.part[...]
    for n in range(1, N_Z):
        source = (place.z + n) % N_Z
        part_copy(layer, place, place.z, source).wait_recv()
        total = total + layer.part_in[source].astype(F32)
    for tap in range(TAPS):
        cols = total[:, tap * GROUP : (tap + 1) * GROUP]
        layer.update[:, tap] = cols.reshape(BANKS, OWN, GROUP)


def finish_delta(layer, place):
    total = layer.diff[...]
    for n in range(1, N_CHAN):
        source = (place.chan + n) % N_CHAN
        diff_copy(layer, place, place.chan, source).wait_recv()
        total = total + layer.diff_in[source].astype(F32)
    layer.delta[...] = total.astype(BF16)


def finish_logit(layer, place, total):
    coefs = layer.coefs[pl.ds(place.batch, 1), :]
    layer.logit[...] = coefs * (total - jnp.sum(coefs * total, axis=1, keepdims=True))


def kernel(*refs):
    args, outs, scratch = refs[:8], refs[8:14], refs[14:]
    fine = Layer(FINE_SIDE, *args[:4], *outs[:3], scratch[:N_LAYER_SCRATCH])
    coarse = Layer(COARSE_SIDE, *args[4:], *outs[3:], scratch[N_LAYER_SCRATCH : 2 * N_LAYER_SCRATCH])
    coef_out, coef_in, totals, coef_ss, coef_rs, total_ss, total_rs = scratch[2 * N_LAYER_SCRATCH :]
    layers = (fine, coarse)
    place = Place()

    barrier = pltpu.get_barrier_semaphore()

    def greet(device):
        pl.semaphore_signal(barrier, inc=1, device_id=device, device_id_type=MESH)

    loop(1, N_XY, lambda n: greet(place.at_xy((place.xy + n) % N_XY)))
    loop(1, N_Z, lambda n: greet(place.at_z((place.z + n) % N_Z)))
    loop(1, N_CHAN, lambda n: greet(place.at_chan((place.chan + n) % N_CHAN)))
    for layer in layers:
        arrange_bank(layer, place)
    shift_upstream(fine)
    pl.semaphore_wait(barrier, N_XY + N_Z + N_CHAN - 3)

    for layer in layers:
        loop(1, N_Z, lambda n: bank_copy(layer, place, (place.z + n) % N_Z, place.z).start())
    send_grads(fine, place)
    shift_upstream(coarse)
    send_grads(coarse, place)
    for layer in layers:
        spread_coefs(layer, place)
    for layer in layers:
        send_kernels(layer, place)
    sums = []
    for layer in layers:
        send_parts(layer, place)
        sums.append(coef_sums(layer)[:, None, :])
    shape = (N_XY, 8, GROUP)
    level = iota(shape, 1)
    both = jnp.where(level == 0, jnp.broadcast_to(sums[0], shape), jnp.broadcast_to(sums[1], shape))
    coef_out[...] = both
    coef_sems = (coef_out, coef_in, coef_ss, coef_rs, place)
    loop(1, N_XY, lambda n: coef_copy(*coef_sems, (place.xy + n) % N_XY, place.xy).start())
    coef_in[place.xy] = coef_out[place.xy]
    for layer in layers:
        send_diffs(layer, place)
    loop(1, N_XY, lambda n: coef_copy(*coef_sems, place.xy, (place.xy + n) % N_XY).wait_recv())
    totals[place.chan] = coef_in[...].sum(axis=0)
    total_sems = (totals, total_ss, total_rs, place)
    loop(1, N_CHAN, lambda n: total_copy(*total_sems, (place.chan + n) % N_CHAN, place.chan).start())
    for layer in layers:
        finish_update(layer, place)
    for layer in layers:
        finish_delta(layer, place)
    loop(1, N_CHAN, lambda n: total_copy(*total_sems, place.chan, (place.chan + n) % N_CHAN).wait_recv())
    total = totals[...].sum(axis=0)
    for index, layer in enumerate(layers):
        finish_logit(layer, place, total[index : index + 1, 0:BANKS])

    for layer in layers:
        loop(1, N_Z, lambda n: bank_copy(layer, place, (place.z + n) % N_Z, place.z).wait_send())
        loop(1, N_XY, lambda n: grad_copy(layer, place, (place.xy + n) % N_XY, place.xy).wait_send())
        loop(1, N_XY, lambda n: kern_copy(layer, place, (place.xy + n) % N_XY, place.xy).wait_send())
        loop(1, N_Z, lambda n: part_copy(layer, place, (place.z + n) % N_Z, place.z).wait_send())
        loop(1, N_CHAN, lambda n: diff_copy(layer, place, (place.chan + n) % N_CHAN, place.chan).wait_send())
    loop(1, N_XY, lambda n: coef_copy(*coef_sems, (place.xy + n) % N_XY, place.xy).wait_send())
    loop(1, N_CHAN, lambda n: total_copy(*total_sems, (place.chan + n) % N_CHAN, place.chan).wait_send())


def per_device(
    fine_inputs,
    fine_upstream,
    fine_bank,
    fine_coefs,
    coarse_inputs,
    coarse_upstream,
    coarse_bank,
    coarse_coefs,
):
    vmem = pl.BlockSpec(memory_space=pltpu.VMEM)
    out_shape = []
    for side in (FINE_SIDE, COARSE_SIDE):
        out_shape += [
            jax.ShapeDtypeStruct((side * side, GROUP), BF16),
            jax.ShapeDtypeStruct((BANKS, TAPS, OWN, GROUP), F32),
            jax.ShapeDtypeStruct((1, BANKS), F32),
        ]
    fine_delta, fine_update, fine_logit, coarse_delta, coarse_update, coarse_logit = pl.pallas_call(
        kernel,
        out_shape=out_shape,
        in_specs=[vmem] * 8,
        out_specs=[vmem] * 6,
        scratch_shapes=layer_scratch(FINE_SIDE)
        + layer_scratch(COARSE_SIDE)
        + [
            pltpu.VMEM((N_XY, 8, GROUP), F32),
            pltpu.VMEM((N_XY, 8, GROUP), F32),
            pltpu.VMEM((N_CHAN, 8, GROUP), F32),
            pltpu.SemaphoreType.DMA((N_XY,)),
            pltpu.SemaphoreType.DMA((N_XY,)),
            pltpu.SemaphoreType.DMA((N_CHAN,)),
            pltpu.SemaphoreType.DMA((N_CHAN,)),
        ],
        compiler_params=pltpu.CompilerParams(
            collective_id=0, has_side_effects=True, vmem_limit_bytes=50 * 1024 * 1024
        ),
    )(
        fine_inputs.reshape(FINE_SIDE * FINE_SIDE, CHANNELS),
        fine_upstream.reshape(FINE_SIDE * FINE_SIDE, GROUP),
        fine_bank,
        fine_coefs,
        coarse_inputs.reshape(COARSE_SIDE * COARSE_SIDE, CHANNELS),
        coarse_upstream.reshape(COARSE_SIDE * COARSE_SIDE, GROUP),
        coarse_bank,
        coarse_coefs,
    )
    return (
        fine_delta.reshape(1, FINE_SIDE, FINE_SIDE, GROUP),
        fine_update,
        fine_logit,
        coarse_delta.reshape(1, COARSE_SIDE, COARSE_SIDE, GROUP),
        coarse_update,
        coarse_logit,
    )


def solution(mesh):
    return jax.shard_map(
        per_device,
        mesh=mesh,
        in_specs=(
            P("batch", None, None, None),
            P("batch", None, None, "chan"),
            P(None, None, "batch", "chan"),
            P(),
            P("batch", None, None, None),
            P("batch", None, None, "chan"),
            P(None, None, "batch", "chan"),
            P(),
        ),
        out_specs=(
            P("batch", None, None, "chan"),
            P(None, None, "batch", "chan"),
            P("batch", None),
            P("batch", None, None, "chan"),
            P(None, None, "batch", "chan"),
            P("batch", None),
        ),
        check_vma=False,
    )
```

```python
import functools

import jax
import jax.numpy as jnp
from jax import lax
from jax.experimental import pallas as pl
from jax.experimental.pallas import tpu as pltpu
from jax.sharding import PartitionSpec as P

BANKS = 8
TAPS = 9
CHANNELS = 512
GROUP = 128
FINE_SIDE = 32
COARSE_SIDE = 16
SAMPLES = 64
N_XY = 16
N_Z = 4
N_CHAN = 4
ROWS = CHANNELS // N_XY
OWN = 8
WIDE = TAPS * GROUP
ROW3 = 3 * GROUP
BLOCK = BANKS * OWN
HALF = BLOCK // 2
BANK_ROWS = N_Z * BLOCK

MIB = 1024 * 1024
MESH = pl.DeviceIdType.MESH
HIGH = lax.Precision.HIGHEST
F32 = jnp.float32
BF16 = jnp.bfloat16


def iota(shape, axis):
    return lax.broadcasted_iota(jnp.int32, shape, axis)


def mm(a, b, contract, precision=None):
    dims = (((contract[0],), (contract[1],)), ((), ()))
    return lax.dot_general(a, b, dims, precision=precision, preferred_element_type=F32)


class Layer:
    def __init__(self, side, args, delta, update, logit, scratch):
        self.side, self.args = side, args
        self.delta, self.update, self.logit = delta, update, logit
        (
            self.inputs, self.upstream, self.bank, self.coefs, self.load_sem,
            self.shifts, self.banks, self.mix, self.back,
            self.grad_out, self.grad_in, self.kern_out, self.kern_in,
            self.part, self.part_out, self.part_in, self.relay, self.diff, self.diff_out, self.diff_in,
            self.bank_ss, self.bank_rs, self.grad_ss, self.grad_rs, self.kern_ss, self.kern_rs,
            self.part_ss, self.part_rs, self.diff_ss, self.diff_rs,
        ) = scratch


def layer_scratch(side):
    pixels = side * side
    return [
        pltpu.VMEM((pixels, CHANNELS), BF16),
        pltpu.VMEM((pixels, GROUP), BF16),
        pltpu.VMEM((BANKS, TAPS, OWN, GROUP), BF16),
        pltpu.VMEM((BANKS, SAMPLES), F32),
        pltpu.SemaphoreType.DMA((4,)),
        pltpu.VMEM((pixels + 2 * side, ROW3), BF16),
        pltpu.VMEM((BANK_ROWS, WIDE), BF16),
        pltpu.VMEM((2, CHANNELS, BANK_ROWS), BF16),
        pltpu.VMEM((2, BANK_ROWS, CHANNELS), BF16),
        pltpu.VMEM((CHANNELS, WIDE), BF16),
        pltpu.VMEM((CHANNELS, WIDE), BF16),
        pltpu.VMEM((CHANNELS, WIDE), BF16),
        pltpu.VMEM((CHANNELS, WIDE), BF16),
        pltpu.VMEM((N_Z, BLOCK, WIDE), F32),
        pltpu.VMEM((N_Z, BLOCK, WIDE), BF16),
        pltpu.VMEM((2, BLOCK, WIDE), BF16),
        pltpu.VMEM((2, HALF, WIDE), BF16),
        pltpu.VMEM((pixels, GROUP), F32),
        pltpu.VMEM((3, pixels, GROUP), BF16),
        pltpu.VMEM((3, pixels, GROUP), BF16),
    ] + [
        pltpu.SemaphoreType.DMA((n,))
        for n in (4, 4, 1, 1, 1, 4, 6, 6, 3, 3)
    ]


N_LAYER_SCRATCH = 30


class Place:
    def __init__(self):
        self.batch = lax.axis_index("batch")
        self.chan = lax.axis_index("chan")
        self.xy = self.batch // N_Z
        self.z = self.batch % N_Z
        self.sibling = self.chan + 1 - 2 * (self.chan % 2)
        self.across = (self.chan + 2) % N_CHAN
        self.corner = (self.sibling + 2) % N_CHAN

    def at_xy(self, xy):
        return (xy * N_Z + self.z, self.chan)

    def at_z(self, z):
        return (self.xy * N_Z + z, self.chan)

    def at_chan(self, chan):
        return (self.batch, chan)


def rows_of(index, count):
    return pl.ds(pl.multiple_of(index * count, count), count)


def bank_copy(layer, place, kind, received=False):
    step = N_Z - 1 if kind % 2 else 1
    origin = place.z if kind < 2 else (place.z + N_Z - step) % N_Z
    if received:
        origin = (origin + N_Z - step) % N_Z
    if kind < 2:
        rows = rows_of(origin, BLOCK)
    else:
        rows = rows_of(2 * origin + kind - 2, HALF)
    return pltpu.make_async_remote_copy(
        src_ref=layer.banks.at[rows],
        dst_ref=layer.banks.at[rows],
        send_sem=layer.bank_ss.at[kind],
        recv_sem=layer.bank_rs.at[kind],
        device_id=place.at_z((place.z + step) % N_Z),
        device_id_type=MESH,
    )


def grad_copy(layer, place, xy_to):
    return pltpu.make_async_remote_copy(
        src_ref=layer.grad_out.at[rows_of(xy_to, ROWS)],
        dst_ref=layer.grad_in.at[rows_of(place.xy, ROWS)],
        send_sem=layer.grad_ss.at[0],
        recv_sem=layer.grad_rs.at[0],
        device_id=place.at_xy(xy_to),
        device_id_type=MESH,
    )


def all_grads(layer, place):
    rows = pl.ds(0, (N_XY - 1) * ROWS)
    return pltpu.make_async_remote_copy(
        src_ref=layer.grad_out.at[rows],
        dst_ref=layer.grad_in.at[rows],
        send_sem=layer.grad_ss.at[0],
        recv_sem=layer.grad_rs.at[0],
        device_id=place.at_xy((place.xy + 1) % N_XY),
        device_id_type=MESH,
    )


def kern_copy(layer, place, xy_to):
    return pltpu.make_async_remote_copy(
        src_ref=layer.kern_out.at[rows_of(xy_to, ROWS)],
        dst_ref=layer.kern_in.at[rows_of(place.xy, ROWS)],
        send_sem=layer.kern_ss.at[0],
        recv_sem=layer.kern_rs.at[place.xy // 4],
        device_id=place.at_xy(xy_to),
        device_id_type=MESH,
    )


def many_kernels(layer, place, y, first, blocks):
    rows = pl.ds(pl.multiple_of(first * ROWS, ROWS), blocks * ROWS)
    return pltpu.make_async_remote_copy(
        src_ref=layer.kern_out.at[rows],
        dst_ref=layer.kern_in.at[rows],
        send_sem=layer.kern_ss.at[0],
        recv_sem=layer.kern_rs.at[y],
        device_id=place.at_xy((place.xy + 1) % N_XY),
        device_id_type=MESH,
    )


def part_copy(layer, place, kind):
    to = (place.z + (1 if kind in (0, 2, 3) else N_Z - 1)) % N_Z
    target = (place.z + 2) % N_Z if kind < 2 else to
    half = (0, 1, 1, 0, 0, 1)[kind]
    rows = pl.ds(half * HALF, HALF)
    if kind < 2:
        landing = layer.relay.at[kind]
    else:
        landing = layer.part_in.at[0 if kind < 4 else 1, rows]
    return pltpu.make_async_remote_copy(
        src_ref=layer.part_out.at[target, rows],
        dst_ref=landing,
        send_sem=layer.part_ss.at[kind],
        recv_sem=layer.part_rs.at[kind],
        device_id=place.at_z(to),
        device_id_type=MESH,
    )


def diff_copy(layer, place, kind):
    return pltpu.make_async_remote_copy(
        src_ref=layer.diff_out.at[kind],
        dst_ref=layer.diff_in.at[kind],
        send_sem=layer.diff_ss.at[kind],
        recv_sem=layer.diff_rs.at[kind],
        device_id=place.at_chan(place.across if kind == 1 else place.sibling),
        device_id_type=MESH,
    )


def coef_copy(out_ref, in_ref, send_sem, recv_sem, place, xy_to):
    return pltpu.make_async_remote_copy(
        src_ref=out_ref.at[xy_to],
        dst_ref=in_ref.at[place.xy],
        send_sem=send_sem.at[0],
        recv_sem=recv_sem.at[0],
        device_id=place.at_xy(xy_to),
        device_id_type=MESH,
    )


def all_coefs(out_ref, in_ref, send_sem, recv_sem, place):
    return pltpu.make_async_remote_copy(
        src_ref=out_ref.at[0 : N_XY - 1],
        dst_ref=in_ref.at[0 : N_XY - 1],
        send_sem=send_sem.at[0],
        recv_sem=recv_sem.at[0],
        device_id=place.at_xy((place.xy + 1) % N_XY),
        device_id_type=MESH,
    )


def total_copy(ref, send_sem, recv_sem, place, chan_to, chan_from):
    return pltpu.make_async_remote_copy(
        src_ref=ref.at[chan_from],
        dst_ref=ref.at[chan_from],
        send_sem=send_sem.at[chan_to],
        recv_sem=recv_sem.at[chan_from],
        device_id=place.at_chan(chan_to),
        device_id_type=MESH,
    )


def loop(low, high, body):
    lax.fori_loop(low, high, lambda n, carry: (body(n), carry)[1], 0)


INPUTS, UPSTREAM, BANK, COEFS = range(4)


def load(layer, which):
    held = (layer.inputs, layer.upstream, layer.bank, layer.coefs)[which]
    return pltpu.make_async_copy(layer.args[which], held, layer.load_sem.at[which])


def arrange_bank(layer, place):
    load(layer, BANK).wait()
    for tap in range(TAPS):
        rows = layer.bank[:, tap].astype(F32).reshape(BLOCK, GROUP).astype(BF16)
        layer.banks[rows_of(place.z, BLOCK), tap * GROUP : (tap + 1) * GROUP] = rows


def shift_upstream(layer):
    load(layer, UPSTREAM).wait()
    side = layer.side
    pixels = side * side
    up = layer.upstream[...].astype(F32)
    column = iota((pixels, GROUP), 0) & (side - 1)
    after = jnp.where(column < side - 1, pltpu.roll(up, pixels - 1, 0), 0.0)
    before = jnp.where(column > 0, pltpu.roll(up, 1, 0), 0.0)
    zeros = jnp.zeros((side, ROW3), BF16)
    layer.shifts[0:side] = zeros
    layer.shifts[side + pixels : 2 * side + pixels] = zeros
    for index, value in enumerate((after, up, before)):
        layer.shifts[side : side + pixels, index * GROUP : (index + 1) * GROUP] = value.astype(BF16)


def window(layer, row_shift):
    start = (2 - row_shift) * layer.side
    return layer.shifts[start : start + layer.side * layer.side]


def split(value, ref):
    hi = value.astype(BF16)
    ref[0] = hi
    ref[1] = (value - hi.astype(F32)).astype(BF16)


def spread_coefs(layer, place):
    load(layer, COEFS).wait()
    bank_rows = BANK_ROWS
    chosen = iota((SAMPLES, N_XY), 0) == iota((SAMPLES, N_XY), 1) * N_Z + place.z
    own = mm(layer.coefs[...], chosen.astype(F32), (1, 0), HIGH)
    col = iota((BANKS, bank_rows), 1)
    wide = mm(own, ((col // OWN) % BANKS == iota((BANKS, bank_rows), 0)).astype(F32), (0, 0), HIGH)
    wide = jnp.broadcast_to(wide[:, None, :], (N_XY, ROWS, bank_rows)).reshape(CHANNELS, bank_rows)
    split(jnp.where(diagonal(), wide, 0.0), layer.mix)
    col = iota((N_XY, CHANNELS), 1)
    tall = mm(own, (col // ROWS == iota((N_XY, CHANNELS), 0)).astype(F32), (1, 0), HIGH)
    tall = jnp.broadcast_to(tall[:, None, :], (BANKS, OWN, CHANNELS)).reshape(BLOCK, CHANNELS)
    tall = jnp.broadcast_to(tall[None], (N_Z, BLOCK, CHANNELS)).reshape(bank_rows, CHANNELS)
    row, col = iota((bank_rows, CHANNELS), 0), iota((bank_rows, CHANNELS), 1)
    same = (row // (BLOCK)) * OWN + row % OWN == col % ROWS
    split(jnp.where(same, tall, 0.0), layer.back)


def diagonal():
    shape = (CHANNELS, BANK_ROWS)
    row, col = iota(shape, 0), iota(shape, 1)
    return row % ROWS == (col // (BLOCK)) * OWN + col % OWN


def send_rows(place, copy):
    my_y = place.xy // 4

    def some(n):
        y = (my_y + n // 4) % 4
        copy(y * 4 + (place.xy + n) % 4).start()

    loop(1, N_XY, some)


def send_grads(layer, place):
    load(layer, INPUTS).wait()

    def chunk(n):
        part = pl.ds(pl.multiple_of(n * 2 * GROUP, 2 * GROUP), 2 * GROUP)
        flipped = layer.inputs[:, part].T
        for row_shift in range(3):
            grad = mm(flipped, window(layer, row_shift), (1, 0)) * (1.0 / layer.side)
            layer.grad_out[part, row_shift * ROW3 : (row_shift + 1) * ROW3] = grad.astype(BF16)

    loop(0, 2, chunk)
    send_rows(place, functools.partial(grad_copy, layer, place))
    own = rows_of(place.xy, ROWS)
    layer.grad_in[own, :] = layer.grad_out[own, :]


def forward_bank(layer, place):
    for kind in (0, 1):
        bank_copy(layer, place, kind, received=True).wait_recv()
        bank_copy(layer, place, kind + 2).start()


def send_kernels(layer, place):
    for kind in (2, 3):
        bank_copy(layer, place, kind, received=True).wait_recv()
    for row_shift in range(3):
        cols = slice(row_shift * ROW3, (row_shift + 1) * ROW3)
        banks = layer.banks[:, cols]

        def chunk(n):
            part = pl.ds(pl.multiple_of(n * 2 * GROUP, 2 * GROUP), 2 * GROUP)
            mixed = mm(layer.mix[0, part], banks, (1, 0)) + mm(layer.mix[1, part], banks, (1, 0))
            layer.kern_out[part, cols] = mixed.astype(BF16)

        loop(0, 2, chunk)
    send_rows(place, functools.partial(kern_copy, layer, place))
    own = rows_of(place.xy, ROWS)
    layer.kern_in[own, :] = layer.kern_out[own, :]


def send_parts(layer, place):
    all_grads(layer, place).wait_recv()
    for row_shift in range(3):
        cols = slice(row_shift * ROW3, (row_shift + 1) * ROW3)
        grads = layer.grad_in[:, cols]
        total = mm(layer.back[0], grads, (1, 0)) + mm(layer.back[1], grads, (1, 0))
        total = total.reshape(N_Z, BLOCK, ROW3)
        layer.part[:, :, cols] = total
        layer.part_out[:, :, cols] = total.astype(BF16)
    for kind in (0, 1, 2, 4):
        part_copy(layer, place, kind).start()


def relay_parts(layer, place):
    for kind, half in ((0, 0), (1, 1)):
        part_copy(layer, place, kind).wait_recv()
        target = (place.z + (1 if kind == 0 else N_Z - 1)) % N_Z
        rows = slice(half * HALF, (half + 1) * HALF)
        total = layer.part[target, rows] + layer.relay[kind].astype(F32)
        layer.part_out[target, rows] = total.astype(BF16)
        part_copy(layer, place, 3 if kind == 0 else 5).start()


def coef_sums(layer):
    bank_rows = BANK_ROWS
    cross = mm(layer.grad_in[...], layer.banks[...], (1, 1))
    cross = jnp.where(diagonal(), cross, 0.0).reshape(N_XY, ROWS, bank_rows).sum(axis=1)
    row = iota((bank_rows, GROUP), 0)
    pick = ((row // OWN) % BANKS == iota((bank_rows, GROUP), 1)).astype(F32)
    return mm(cross, pick, (1, 0), HIGH)


def diff_of(layer, place, chan):
    y, my_y = chan, place.xy // 4

    @pl.when(y != my_y)
    def _():
        many_kernels(layer, place, y, y * 4, 4).wait_recv()

    @pl.when(y == my_y)
    def _():
        many_kernels(layer, place, y, y * 4, 3).wait_recv()

    part = pl.ds(pl.multiple_of(chan * GROUP, GROUP), GROUP)
    diff = mm(window(layer, 0), layer.kern_in[part, 0:ROW3], (1, 1))
    for row_shift in (1, 2):
        cols = slice(row_shift * ROW3, (row_shift + 1) * ROW3)
        diff = diff + mm(window(layer, row_shift), layer.kern_in[part, cols], (1, 1))
    layer.diff[...] = diff


def send_diffs(layer, place):
    diff_of(layer, place, place.corner)
    layer.diff_out[0] = layer.diff[...].astype(BF16)
    diff_copy(layer, place, 0).start()
    diff_of(layer, place, place.across)
    diff_copy(layer, place, 0).wait_recv()
    layer.diff_out[1] = (layer.diff[...] + layer.diff_in[0].astype(F32)).astype(BF16)
    diff_copy(layer, place, 1).start()
    diff_of(layer, place, place.sibling)
    layer.diff_out[2] = layer.diff[...].astype(BF16)
    diff_copy(layer, place, 2).start()
    diff_of(layer, place, place.chan)


def finish_update(layer, place):
    for kind in (2, 3, 4, 5):
        part_copy(layer, place, kind).wait_recv()
    total = layer.part[place.z] + layer.part_in[0].astype(F32) + layer.part_in[1].astype(F32)
    for tap in range(TAPS):
        cols = total[:, tap * GROUP : (tap + 1) * GROUP]
        layer.update[:, tap] = cols.reshape(BANKS, OWN, GROUP)


def finish_delta(layer, place):
    total = layer.diff[...]
    for kind in (2, 1):
        diff_copy(layer, place, kind).wait_recv()
        total = total + layer.diff_in[kind].astype(F32)
    layer.delta[...] = total.astype(BF16)


def finish_logit(layer, place, total):
    chosen = (iota((1, SAMPLES), 1) == place.batch).astype(F32)
    coefs = mm(chosen, layer.coefs[...], (1, 1), HIGH)
    layer.logit[...] = coefs * (total - jnp.sum(coefs * total, axis=1, keepdims=True))


def kernel(*refs):
    args, outs, scratch = refs[:8], refs[8:14], refs[14:]
    fine = Layer(FINE_SIDE, args[:4], *outs[:3], scratch[:N_LAYER_SCRATCH])
    coarse = Layer(COARSE_SIDE, args[4:], *outs[3:], scratch[N_LAYER_SCRATCH : 2 * N_LAYER_SCRATCH])
    coef_out, coef_in, totals, coef_ss, coef_rs, total_ss, total_rs = scratch[2 * N_LAYER_SCRATCH :]
    layers = (fine, coarse)
    place = Place()

    for which in (BANK, UPSTREAM, INPUTS, COEFS):
        for layer in layers:
            load(layer, which).start()
    barrier = pltpu.get_barrier_semaphore()

    def greet(device):
        pl.semaphore_signal(barrier, inc=1, device_id=device, device_id_type=MESH)

    loop(1, N_XY, lambda n: greet(place.at_xy((place.xy + n) % N_XY)))
    for step in (1, N_Z - 1):
        greet(place.at_z((place.z + step) % N_Z))
    loop(1, N_CHAN, lambda n: greet(place.at_chan((place.chan + n) % N_CHAN)))
    for layer in layers:
        arrange_bank(layer, place)
    shift_upstream(fine)
    pl.semaphore_wait(barrier, N_XY + N_CHAN)

    for layer in layers:
        for kind in (0, 1):
            bank_copy(layer, place, kind).start()
    send_grads(fine, place)
    forward_bank(fine, place)
    shift_upstream(coarse)
    send_grads(coarse, place)
    forward_bank(coarse, place)
    for layer in layers:
        spread_coefs(layer, place)
    for layer in layers:
        send_kernels(layer, place)
    send_parts(fine, place)
    fine_sums = coef_sums(fine)
    send_parts(coarse, place)
    relay_parts(fine, place)
    coarse_sums = coef_sums(coarse)
    shape = (N_XY, 8, GROUP)
    wide_sums = [jnp.broadcast_to(sums[:, None, :], shape) for sums in (fine_sums, coarse_sums)]
    coef_out[...] = jnp.where(iota(shape, 1) == 0, *wide_sums)
    coef_refs = (coef_out, coef_in, coef_ss, coef_rs, place)
    loop(1, N_XY, lambda n: coef_copy(*coef_refs, (place.xy + n) % N_XY).start())
    coef_in[place.xy] = coef_out[place.xy]
    relay_parts(coarse, place)
    all_coefs(*coef_refs).wait_recv()
    totals[place.chan] = coef_in[...].sum(axis=0)
    total_refs = (totals, total_ss, total_rs, place)
    loop(1, N_CHAN, lambda n: total_copy(*total_refs, (place.chan + n) % N_CHAN, place.chan).start())
    send_diffs(fine, place)
    for layer in layers:
        finish_update(layer, place)
    loop(1, N_CHAN, lambda n: total_copy(*total_refs, place.chan, (place.chan + n) % N_CHAN).wait_recv())
    total = totals[...].sum(axis=0)
    for index, layer in enumerate(layers):
        finish_logit(layer, place, total[index : index + 1, 0:BANKS])
    send_diffs(coarse, place)
    for layer in layers:
        finish_delta(layer, place)

    for layer in layers:
        for kind in range(4):
            bank_copy(layer, place, kind).wait_send()
        for kind in range(6):
            part_copy(layer, place, kind).wait_send()
        for kind in range(3):
            diff_copy(layer, place, kind).wait_send()
        all_grads(layer, place).wait_send()
        many_kernels(layer, place, 0, 0, N_XY - 1).wait_send()
    all_coefs(*coef_refs).wait_send()
    loop(1, N_CHAN, lambda n: total_copy(*total_refs, (place.chan + n) % N_CHAN, place.chan).wait_send())


def store(*refs):
    given, out, held, (in_sem, out_sem) = refs[:6], refs[6:12], refs[12:18], refs[18:]
    loads = [pltpu.make_async_copy(given[n], held[n], in_sem.at[n]) for n in range(6)]
    stores = [pltpu.make_async_copy(held[n], out[n], out_sem.at[n]) for n in range(6)]
    for copy in loads:
        copy.start()
    for first, second in zip(loads, stores):
        first.wait()
        second.start()
    for copy in stores:
        copy.wait()


def per_device(
    fine_inputs,
    fine_upstream,
    fine_bank,
    fine_coefs,
    coarse_inputs,
    coarse_upstream,
    coarse_bank,
    coarse_coefs,
):
    vmem = pl.BlockSpec(memory_space=pltpu.VMEM)
    hbm = pl.BlockSpec(memory_space=pltpu.HBM)
    out_shape = []
    for side in (FINE_SIDE, COARSE_SIDE):
        out_shape += [
            jax.ShapeDtypeStruct((side * side, GROUP), BF16),
            jax.ShapeDtypeStruct((BANKS, TAPS, OWN, GROUP), F32),
            jax.ShapeDtypeStruct((1, BANKS), F32),
        ]
    results = pl.pallas_call(
        kernel,
        out_shape=out_shape,
        in_specs=[hbm] * 8,
        out_specs=[vmem] * 6,
        scratch_shapes=layer_scratch(FINE_SIDE)
        + layer_scratch(COARSE_SIDE)
        + [
            pltpu.VMEM((N_XY, 8, GROUP), F32),
            pltpu.VMEM((N_XY, 8, GROUP), F32),
            pltpu.VMEM((N_CHAN, 8, GROUP), F32),
            pltpu.SemaphoreType.DMA((1,)),
            pltpu.SemaphoreType.DMA((1,)),
            pltpu.SemaphoreType.DMA((N_CHAN,)),
            pltpu.SemaphoreType.DMA((N_CHAN,)),
        ],
        compiler_params=pltpu.CompilerParams(
            collective_id=0, has_side_effects=True, vmem_limit_bytes=62 * MIB
        ),
    )(
        fine_inputs.reshape(FINE_SIDE * FINE_SIDE, CHANNELS),
        fine_upstream.reshape(FINE_SIDE * FINE_SIDE, GROUP),
        fine_bank,
        fine_coefs.T,
        coarse_inputs.reshape(COARSE_SIDE * COARSE_SIDE, CHANNELS),
        coarse_upstream.reshape(COARSE_SIDE * COARSE_SIDE, GROUP),
        coarse_bank,
        coarse_coefs.T,
    )
    fine_delta, fine_update, fine_logit, coarse_delta, coarse_update, coarse_logit = pl.pallas_call(
        store,
        out_shape=out_shape,
        in_specs=[hbm] * 6,
        out_specs=[hbm] * 6,
        scratch_shapes=[pltpu.VMEM(out.shape, out.dtype) for out in out_shape]
        + [pltpu.SemaphoreType.DMA((6,)), pltpu.SemaphoreType.DMA((6,))],
        compiler_params=pltpu.CompilerParams(vmem_limit_bytes=62 * MIB),
    )(*results)
    return (
        fine_delta.reshape(1, FINE_SIDE, FINE_SIDE, GROUP),
        fine_update,
        fine_logit,
        coarse_delta.reshape(1, COARSE_SIDE, COARSE_SIDE, GROUP),
        coarse_update,
        coarse_logit,
    )


def solution(mesh):
    return jax.shard_map(
        per_device,
        mesh=mesh,
        in_specs=(
            P("batch", None, None, None),
            P("batch", None, None, "chan"),
            P(None, None, "batch", "chan"),
            P(),
            P("batch", None, None, None),
            P("batch", None, None, "chan"),
            P(None, None, "batch", "chan"),
            P(),
        ),
        out_specs=(
            P("batch", None, None, "chan"),
            P(None, None, "batch", "chan"),
            P("batch", None),
            P("batch", None, None, "chan"),
            P(None, None, "batch", "chan"),
            P("batch", None),
        ),
        check_vma=False,
    )
```

```python
import functools

import jax
import jax.numpy as jnp
from jax import lax
from jax.experimental import pallas as pl
from jax.experimental.pallas import tpu as pltpu
from jax.sharding import PartitionSpec as P

BANKS = 8
TAPS = 9
CHANNELS = 512
GROUP = 128
FINE_SIDE = 32
COARSE_SIDE = 16
STEP = 128
AT_ONCE = 4
SAMPLES = 64
N_XY = 16
N_Z = 4
N_CHAN = 4
ROWS = CHANNELS // N_XY
OWN = 8
WIDE = TAPS * GROUP
ROW3 = 3 * GROUP
BLOCK = BANKS * OWN
HALF = BLOCK // 2
BANK_ROWS = N_Z * BLOCK

MIB = 1024 * 1024
MESH = pl.DeviceIdType.MESH
HIGH = lax.Precision.HIGHEST
F32 = jnp.float32
BF16 = jnp.bfloat16


def iota(shape, axis):
    return lax.broadcasted_iota(jnp.int32, shape, axis)


def mm(a, b, contract, precision=None):
    dims = (((contract[0],), (contract[1],)), ((), ()))
    return lax.dot_general(a, b, dims, precision=precision, preferred_element_type=F32)


class Layer:
    def __init__(self, side, args, delta, update, logit, scratch):
        self.side, self.args = side, args
        self.delta, self.update, self.logit = delta, update, logit
        (
            self.inputs, self.upstream, self.bank, self.coefs, self.load_sem,
            self.shifts, self.flipped, self.spread, self.cross, self.banks, self.mix, self.back,
            self.grad_out, self.grad_in, self.kern_out, self.kern_in,
            self.part, self.part_out, self.part_in, self.relay, self.diff, self.diff_out, self.diff_in,
            self.bank_ss, self.bank_rs, self.grad_ss, self.grad_rs, self.kern_ss, self.kern_rs,
            self.part_ss, self.part_rs, self.diff_ss, self.diff_rs,
        ) = scratch


def layer_scratch(side):
    pixels = side * side
    diff = (pixels, GROUP) if side == FINE_SIDE else (GROUP, pixels)
    return [
        pltpu.VMEM((pixels, CHANNELS), BF16),
        pltpu.VMEM((pixels, GROUP), BF16),
        pltpu.VMEM((BANKS, TAPS, OWN, GROUP), BF16),
        pltpu.VMEM((BANKS, SAMPLES), F32),
        pltpu.SemaphoreType.DMA((4,)),
        pltpu.VMEM((pixels + 2 * side, ROW3), BF16),
        pltpu.VMEM((CHANNELS, pixels), BF16),
        pltpu.VMEM((N_XY, BANK_ROWS), F32),
        pltpu.VMEM((N_XY, BANK_ROWS), F32),
        pltpu.VMEM((BANK_ROWS, WIDE), BF16),
        pltpu.VMEM((2, CHANNELS, BANK_ROWS), BF16),
        pltpu.VMEM((2, BANK_ROWS, CHANNELS), BF16),
        pltpu.VMEM((CHANNELS, WIDE), BF16),
        pltpu.VMEM((CHANNELS, WIDE), BF16),
        pltpu.VMEM((CHANNELS, WIDE), BF16),
        pltpu.VMEM((CHANNELS, WIDE), BF16),
        pltpu.VMEM((N_Z, BLOCK, WIDE), F32),
        pltpu.VMEM((N_Z, BLOCK, WIDE), BF16),
        pltpu.VMEM((2, BLOCK, WIDE), BF16),
        pltpu.VMEM((2, HALF, WIDE), BF16),
        pltpu.VMEM(diff, F32),
        pltpu.VMEM((3, *diff), BF16),
        pltpu.VMEM((3, *diff), BF16),
    ] + [
        pltpu.SemaphoreType.DMA((n,))
        for n in (4, 4, 1, 1, 1, 4, 6, 6, 3, 3)
    ]


N_LAYER_SCRATCH = 33


class Place:
    def __init__(self):
        self.batch = lax.axis_index("batch")
        self.chan = lax.axis_index("chan")
        self.xy = self.batch // N_Z
        self.z = self.batch % N_Z
        self.sibling = self.chan + 1 - 2 * (self.chan % 2)
        self.across = (self.chan + 2) % N_CHAN

    def at_xy(self, xy):
        return (xy * N_Z + self.z, self.chan)

    def at_z(self, z):
        return (self.xy * N_Z + z, self.chan)

    def at_chan(self, chan):
        return (self.batch, chan)


def rows_of(index, count):
    return pl.ds(pl.multiple_of(index * count, count), count)


def bank_copy(layer, place, kind, received=False):
    step = N_Z - 1 if kind % 2 else 1
    origin = place.z if kind < 2 else (place.z + N_Z - step) % N_Z
    if received:
        origin = (origin + N_Z - step) % N_Z
    if kind < 2:
        rows = rows_of(origin, BLOCK)
    else:
        rows = rows_of(2 * origin + kind - 2, HALF)
    return pltpu.make_async_remote_copy(
        src_ref=layer.banks.at[rows],
        dst_ref=layer.banks.at[rows],
        send_sem=layer.bank_ss.at[kind],
        recv_sem=layer.bank_rs.at[kind],
        device_id=place.at_z((place.z + step) % N_Z),
        device_id_type=MESH,
    )


def grad_copy(layer, place, xy_to):
    return pltpu.make_async_remote_copy(
        src_ref=layer.grad_out.at[rows_of(xy_to, ROWS)],
        dst_ref=layer.grad_in.at[rows_of(place.xy, ROWS)],
        send_sem=layer.grad_ss.at[0],
        recv_sem=layer.grad_rs.at[0],
        device_id=place.at_xy(xy_to),
        device_id_type=MESH,
    )


def all_grads(layer, place):
    rows = pl.ds(0, (N_XY - 1) * ROWS)
    return pltpu.make_async_remote_copy(
        src_ref=layer.grad_out.at[rows],
        dst_ref=layer.grad_in.at[rows],
        send_sem=layer.grad_ss.at[0],
        recv_sem=layer.grad_rs.at[0],
        device_id=place.at_xy((place.xy + 1) % N_XY),
        device_id_type=MESH,
    )


def kern_copy(layer, place, xy_to):
    return pltpu.make_async_remote_copy(
        src_ref=layer.kern_out.at[rows_of(xy_to, ROWS)],
        dst_ref=layer.kern_in.at[rows_of(place.xy, ROWS)],
        send_sem=layer.kern_ss.at[0],
        recv_sem=layer.kern_rs.at[place.xy // 4],
        device_id=place.at_xy(xy_to),
        device_id_type=MESH,
    )


def many_kernels(layer, place, y, first, blocks):
    rows = pl.ds(pl.multiple_of(first * ROWS, ROWS), blocks * ROWS)
    return pltpu.make_async_remote_copy(
        src_ref=layer.kern_out.at[rows],
        dst_ref=layer.kern_in.at[rows],
        send_sem=layer.kern_ss.at[0],
        recv_sem=layer.kern_rs.at[y],
        device_id=place.at_xy((place.xy + 1) % N_XY),
        device_id_type=MESH,
    )


def part_copy(layer, place, kind):
    to = (place.z + (1 if kind in (0, 2, 3) else N_Z - 1)) % N_Z
    target = (place.z + 2) % N_Z if kind < 2 else to
    half = (0, 1, 1, 0, 0, 1)[kind]
    rows = pl.ds(half * HALF, HALF)
    if kind < 2:
        landing = layer.relay.at[kind]
    else:
        landing = layer.part_in.at[0 if kind < 4 else 1, rows]
    return pltpu.make_async_remote_copy(
        src_ref=layer.part_out.at[target, rows],
        dst_ref=landing,
        send_sem=layer.part_ss.at[kind],
        recv_sem=layer.part_rs.at[kind],
        device_id=place.at_z(to),
        device_id_type=MESH,
    )


def diff_copy(layer, place, kind):
    return pltpu.make_async_remote_copy(
        src_ref=layer.diff_out.at[kind],
        dst_ref=layer.diff_in.at[kind],
        send_sem=layer.diff_ss.at[kind],
        recv_sem=layer.diff_rs.at[kind],
        device_id=place.at_chan(place.across if kind == 1 else place.sibling),
        device_id_type=MESH,
    )


def coef_copy(out_ref, in_ref, send_sem, recv_sem, place, xy_to):
    return pltpu.make_async_remote_copy(
        src_ref=out_ref.at[xy_to],
        dst_ref=in_ref.at[place.xy],
        send_sem=send_sem.at[0],
        recv_sem=recv_sem.at[0],
        device_id=place.at_xy(xy_to),
        device_id_type=MESH,
    )


def all_coefs(out_ref, in_ref, send_sem, recv_sem, place):
    return pltpu.make_async_remote_copy(
        src_ref=out_ref.at[0 : N_XY - 1],
        dst_ref=in_ref.at[0 : N_XY - 1],
        send_sem=send_sem.at[0],
        recv_sem=recv_sem.at[0],
        device_id=place.at_xy((place.xy + 1) % N_XY),
        device_id_type=MESH,
    )


def total_copy(ref, send_sem, recv_sem, place, chan_to, chan_from):
    return pltpu.make_async_remote_copy(
        src_ref=ref.at[chan_from],
        dst_ref=ref.at[chan_from],
        send_sem=send_sem.at[chan_to],
        recv_sem=recv_sem.at[chan_from],
        device_id=place.at_chan(chan_to),
        device_id_type=MESH,
    )


def loop(low, high, body):
    lax.fori_loop(low, high, lambda n, carry: (body(n), carry)[1], 0)


INPUTS, UPSTREAM, BANK, COEFS = range(4)


def load(layer, which):
    held = (layer.inputs, layer.upstream, layer.bank, layer.coefs)[which]
    return pltpu.make_async_copy(layer.args[which], held, layer.load_sem.at[which])


def arrange_bank(layer, place):
    load(layer, BANK).wait()

    def move(tap):
        rows = layer.bank[:, tap].astype(F32).reshape(BLOCK, GROUP).astype(BF16)
        layer.banks[rows_of(place.z, BLOCK), rows_of(tap, GROUP)] = rows

    loop(0, TAPS, move)


def clear_edges(shifts, side):
    zeros = jnp.zeros((side, ROW3), BF16)
    shifts[0:side] = zeros
    shifts[shifts.shape[0] - side : shifts.shape[0]] = zeros


def shift_rows(upstream, shifts, side, n):
    column = iota((STEP, GROUP), 0) & (side - 1)
    up = upstream[rows_of(n, STEP)].astype(F32)
    after = jnp.where(column < side - 1, pltpu.roll(up, STEP - 1, 0), 0.0)
    before = jnp.where(column > 0, pltpu.roll(up, 1, 0), 0.0)
    rows = pl.ds(pl.multiple_of(n * STEP + side, side), STEP)
    for index, value in enumerate((after, up, before)):
        shifts[rows, index * GROUP : (index + 1) * GROUP] = value.astype(BF16)


def shift_upstream(layer):
    load(layer, UPSTREAM).wait()
    clear_edges(layer.shifts, layer.side)
    loop(0, layer.side * layer.side // STEP, lambda n: shift_rows(layer.upstream, layer.shifts, layer.side, n))


def window(layer, row_shift, first, count):
    start = pl.multiple_of((2 - row_shift) * layer.side + first, layer.side)
    return layer.shifts[pl.ds(start, count)]


def split(value, ref, rows):
    hi = value.astype(BF16)
    ref[0, rows] = hi
    ref[1, rows] = (value - hi.astype(F32)).astype(BF16)


def spread_coefs(layer, place):
    load(layer, COEFS).wait()
    chosen = iota((SAMPLES, N_XY), 0) == iota((SAMPLES, N_XY), 1) * N_Z + place.z
    own = mm(layer.coefs[...], chosen.astype(F32), (1, 0), HIGH)
    col = iota((BANKS, BANK_ROWS), 1)
    wide = ((col // OWN) % BANKS == iota((BANKS, BANK_ROWS), 0)).astype(F32)
    layer.spread[...] = mm(own, wide, (0, 0), HIGH)
    same = diagonal(ROWS)

    def sample(n):
        row = jnp.broadcast_to(layer.spread[pl.ds(n, 1), :], (ROWS, BANK_ROWS))
        split(jnp.where(same, row, 0.0), layer.mix, rows_of(n, ROWS))

    loop(0, N_XY, sample)
    col = iota((N_XY, CHANNELS), 1)
    tall = mm(own, (col // ROWS == iota((N_XY, CHANNELS), 0)).astype(F32), (1, 0), HIGH)
    tall = jnp.broadcast_to(tall[:, None, :], (BANKS, OWN, CHANNELS)).reshape(BLOCK, CHANNELS)
    row, col = iota((BLOCK, CHANNELS), 0), iota((BLOCK, CHANNELS), 1)

    def block(n):
        same = n * OWN + row % OWN == col % ROWS
        split(jnp.where(same, tall, 0.0), layer.back, rows_of(n, BLOCK))

    loop(0, N_Z, block)


def diagonal(rows):
    shape = (rows, BANK_ROWS)
    row, col = iota(shape, 0), iota(shape, 1)
    return row % ROWS == (col // BLOCK) * OWN + col % OWN


AROUND = (
    (1, 0), (0, 1), (3, 0), (0, 3), (1, 1), (3, 3), (2, 0), (0, 2),
    (1, 3), (3, 1), (2, 1), (2, 3), (1, 2), (3, 2), (2, 2),
)


def send_rows(place, copy):
    y, x = place.xy // 4, place.xy % 4
    for step_x, step_y in AROUND:
        copy((y + step_y) % 4 * 4 + (x + step_x) % 4).start()


def flip_inputs(layer):
    load(layer, INPUTS).wait()

    def flip(n):
        layer.flipped[rows_of(n, GROUP)] = layer.inputs[:, rows_of(n, GROUP)].T

    loop(0, CHANNELS // GROUP, flip)


def send_grads(layer, place):
    flip_inputs(layer)
    pixels = layer.side * layer.side

    def chunk(n):
        row_shift, part = n // 2, rows_of(n % 2, 2 * GROUP)
        grad = mm(layer.flipped[part], window(layer, row_shift, 0, pixels), (1, 0)) * (1.0 / layer.side)
        layer.grad_out[part, rows_of(row_shift, ROW3)] = grad.astype(BF16)

    loop(0, 6, chunk)
    send_rows(place, functools.partial(grad_copy, layer, place))
    own = rows_of(place.xy, ROWS)
    layer.grad_in[own, :] = layer.grad_out[own, :]


def forward_bank(layer, place):
    for kind in (0, 1):
        bank_copy(layer, place, kind, received=True).wait_recv()
        bank_copy(layer, place, kind + 2).start()


def mix_kernels(layer, place):
    for kind in (2, 3):
        bank_copy(layer, place, kind, received=True).wait_recv()

    def chunk(n):
        cols, part = rows_of(n // 2, ROW3), rows_of(n % 2, 2 * GROUP)
        banks = layer.banks[:, cols]
        mixed = mm(layer.mix[0, part], banks, (1, 0)) + mm(layer.mix[1, part], banks, (1, 0))
        layer.kern_out[part, cols] = mixed.astype(BF16)

    loop(0, 6, chunk)


def send_kernels(layer, place):
    mix_kernels(layer, place)
    send_rows(place, functools.partial(kern_copy, layer, place))
    own = rows_of(place.xy, ROWS)
    layer.kern_in[own, :] = layer.kern_out[own, :]


class Samples:
    def __init__(self, layer, place, scratch):
        self.layer, self.place = layer, place
        (
            self.upstream, self.inputs, self.shifts, self.diff_out, self.diff_in,
            self.up_ss, self.up_rs, self.in_ss, self.in_rs, self.diff_ss, self.diff_rs,
        ) = scratch

    def copy(self, source, target, send_sem, recv_sem, to):
        return pltpu.make_async_remote_copy(
            src_ref=source,
            dst_ref=target,
            send_sem=send_sem.at[0],
            recv_sem=recv_sem.at[0],
            device_id=self.place.at_xy(to),
            device_id_type=MESH,
        )

    def up_copy(self, to):
        return self.copy(self.layer.upstream, self.upstream.at[self.place.xy], self.up_ss, self.up_rs, to)

    def in_copy(self, to):
        rows, here = rows_of(to, ROWS), rows_of(self.place.xy, ROWS)
        return self.copy(self.layer.flipped.at[rows], self.inputs.at[here], self.in_ss, self.in_rs, to)

    def diff_copy(self, to):
        rows, here = rows_of(to, ROWS), rows_of(self.place.xy, ROWS)
        return self.copy(self.diff_out.at[rows], self.diff_in.at[here], self.diff_ss, self.diff_rs, to)

    def all_copies(self):
        to = (self.place.xy + 1) % N_XY
        some, rows = pl.ds(0, N_XY - 1), pl.ds(0, (N_XY - 1) * ROWS)
        return (
            self.copy(self.upstream.at[some], self.upstream.at[some], self.up_ss, self.up_rs, to),
            self.copy(self.layer.flipped.at[rows], self.inputs.at[rows], self.in_ss, self.in_rs, to),
            self.copy(self.diff_out.at[rows], self.diff_in.at[rows], self.diff_ss, self.diff_rs, to),
        )

    def send(self):
        place, own = self.place, rows_of(self.place.xy, ROWS)
        load(self.layer, UPSTREAM).wait()
        send_rows(place, self.up_copy)
        flip_inputs(self.layer)
        send_rows(place, self.in_copy)
        self.upstream[place.xy] = self.layer.upstream[...]
        self.inputs[own] = self.layer.flipped[own]

    def work(self):
        layer, place, side = self.layer, self.place, self.layer.side
        pixels = side * side
        for at in range(AT_ONCE):
            clear_edges(self.shifts.at[at], side)
        for copy in self.all_copies()[:2]:
            copy.wait_recv()

        def some(n):
            for at in range(AT_ONCE):
                for part in range(pixels // STEP):
                    shift_rows(self.upstream.at[n * AT_ONCE + at], self.shifts.at[at], side, part)
            for at in range(AT_ONCE):
                rows = rows_of(n * AT_ONCE + at, ROWS)
                inputs, diff = self.inputs[rows], None
                for row_shift in range(3):
                    cols = slice(row_shift * ROW3, (row_shift + 1) * ROW3)
                    start = (2 - row_shift) * side
                    shifted = self.shifts[at, start : start + pixels]
                    grad = mm(inputs, shifted, (1, 0)) * (1.0 / side)
                    layer.grad_in[rows, cols] = grad.astype(BF16)
                    term = mm(layer.kern_out[rows, cols], shifted, (1, 1))
                    diff = term if diff is None else diff + term
                self.diff_out[rows] = diff.astype(BF16)

        loop(0, N_XY // AT_ONCE, some)
        send_rows(place, self.diff_copy)
        own = rows_of(place.xy, ROWS)
        self.diff_in[own] = self.diff_out[own]


def send_parts(layer, place):
    def some(n):
        cols = rows_of(n, ROW3)
        grads = layer.grad_in[:, cols]
        total = mm(layer.back[0], grads, (1, 0)) + mm(layer.back[1], grads, (1, 0))
        total = total.reshape(N_Z, BLOCK, ROW3)
        layer.part[:, :, cols] = total
        layer.part_out[:, :, cols] = total.astype(BF16)

    loop(0, 3, some)
    for kind in (0, 1, 2, 4):
        part_copy(layer, place, kind).start()


def relay_parts(layer, place):
    for kind, half in ((0, 0), (1, 1)):
        part_copy(layer, place, kind).wait_recv()
        target = (place.z + (1 if kind == 0 else N_Z - 1)) % N_Z
        rows = slice(half * HALF, (half + 1) * HALF)
        total = layer.part[target, rows] + layer.relay[kind].astype(F32)
        layer.part_out[target, rows] = total.astype(BF16)
        part_copy(layer, place, 3 if kind == 0 else 5).start()


def coef_sums(layer):
    same = diagonal(STEP)

    def some(n):
        cross = mm(layer.grad_in[rows_of(n, STEP)], layer.banks[...], (1, 1))
        cross = jnp.where(same, cross, 0.0).reshape(STEP // ROWS, ROWS, BANK_ROWS).sum(axis=1)
        for sample in range(STEP // ROWS):
            layer.cross[pl.ds(n * (STEP // ROWS) + sample, 1), :] = cross[sample : sample + 1]

    loop(0, CHANNELS // STEP, some)
    row = iota((BANK_ROWS, GROUP), 0)
    pick = ((row // OWN) % BANKS == iota((BANK_ROWS, GROUP), 1)).astype(F32)
    return mm(layer.cross[...], pick, (1, 0), HIGH)


def diff_of(layer, place, chan):
    y, my_y = chan, place.xy // 4

    @pl.when(y != my_y)
    def _():
        many_kernels(layer, place, y, y * 4, 4).wait_recv()

    @pl.when(y == my_y)
    def _():
        many_kernels(layer, place, y, y * 4, 3).wait_recv()

    part, size = rows_of(chan, GROUP), 2 * STEP

    def some(n):
        diff = mm(window(layer, 0, n * size, size), layer.kern_in[part, 0:ROW3], (1, 1))
        for row_shift in (1, 2):
            cols = slice(row_shift * ROW3, (row_shift + 1) * ROW3)
            diff = diff + mm(window(layer, row_shift, n * size, size), layer.kern_in[part, cols], (1, 1))
        layer.diff[rows_of(n, size)] = diff

    loop(0, layer.side * layer.side // size, some)


def send_diffs(layer, place, diff_of):
    def target(n):
        base = (place.chan + 2 * (1 - n // 2)) % N_CHAN
        diff_of(base + (1 - n % 2) * (1 - 2 * (place.chan % 2)))

        @pl.when(n == 0)
        def _():
            layer.diff_out[0] = layer.diff[...].astype(BF16)
            diff_copy(layer, place, 0).start()

        @pl.when(n == 1)
        def _():
            diff_copy(layer, place, 0).wait_recv()
            layer.diff_out[1] = (layer.diff[...] + layer.diff_in[0].astype(F32)).astype(BF16)
            diff_copy(layer, place, 1).start()

        @pl.when(n == 2)
        def _():
            layer.diff_out[2] = layer.diff[...].astype(BF16)
            diff_copy(layer, place, 2).start()

    loop(0, N_CHAN, target)


def finish_update(layer, place):
    for kind in (2, 3, 4, 5):
        part_copy(layer, place, kind).wait_recv()
    total = layer.part[place.z] + layer.part_in[0].astype(F32) + layer.part_in[1].astype(F32)
    for tap in range(TAPS):
        cols = total[:, tap * GROUP : (tap + 1) * GROUP]
        layer.update[:, tap] = cols.reshape(BANKS, OWN, GROUP)


def finish_delta(layer, place):
    total = layer.diff[...]
    for kind in (2, 1):
        diff_copy(layer, place, kind).wait_recv()
        total = total + layer.diff_in[kind].astype(F32)
    layer.delta[...] = (total if layer.side == FINE_SIDE else total.T).astype(BF16)


def finish_logit(layer, place, total):
    chosen = (iota((1, SAMPLES), 1) == place.batch).astype(F32)
    coefs = mm(chosen, layer.coefs[...], (1, 1), HIGH)
    layer.logit[...] = coefs * (total - jnp.sum(coefs * total, axis=1, keepdims=True))


def kernel(*refs):
    args, outs, scratch = refs[:8], refs[8:14], refs[14:]
    fine = Layer(FINE_SIDE, args[:4], *outs[:3], scratch[:N_LAYER_SCRATCH])
    coarse = Layer(COARSE_SIDE, args[4:], *outs[3:], scratch[N_LAYER_SCRATCH : 2 * N_LAYER_SCRATCH])
    coef_out, coef_in, totals, coef_ss, coef_rs, total_ss, total_rs, *rest = scratch[2 * N_LAYER_SCRATCH :]
    layers = (fine, coarse)
    place = Place()
    samples = Samples(coarse, place, rest)

    for which in (BANK, UPSTREAM, INPUTS, COEFS):
        for layer in layers:
            load(layer, which).start()
    barrier = pltpu.get_barrier_semaphore()

    def greet(device):
        pl.semaphore_signal(barrier, inc=1, device_id=device, device_id_type=MESH)

    loop(1, N_XY, lambda n: greet(place.at_xy((place.xy + n) % N_XY)))
    for step in (1, N_Z - 1):
        greet(place.at_z((place.z + step) % N_Z))
    loop(1, N_CHAN, lambda n: greet(place.at_chan((place.chan + n) % N_CHAN)))
    for layer in layers:
        arrange_bank(layer, place)
    shift_upstream(fine)
    pl.semaphore_wait(barrier, N_XY + N_CHAN)

    for layer in layers:
        for kind in (0, 1):
            bank_copy(layer, place, kind).start()
    samples.send()
    send_grads(fine, place)
    for layer in layers:
        forward_bank(layer, place)
    for layer in layers:
        spread_coefs(layer, place)
    send_kernels(fine, place)
    mix_kernels(coarse, place)
    samples.work()
    send_parts(coarse, place)
    coarse_sums = coef_sums(coarse)
    all_grads(fine, place).wait_recv()
    send_parts(fine, place)
    relay_parts(coarse, place)
    fine_sums = coef_sums(fine)
    shape = (N_XY, 8, GROUP)
    wide_sums = [jnp.broadcast_to(sums[:, None, :], shape) for sums in (fine_sums, coarse_sums)]
    coef_out[...] = jnp.where(iota(shape, 1) == 0, *wide_sums)
    coef_refs = (coef_out, coef_in, coef_ss, coef_rs, place)
    loop(1, N_XY, lambda n: coef_copy(*coef_refs, (place.xy + n) % N_XY).start())
    coef_in[place.xy] = coef_out[place.xy]
    relay_parts(fine, place)
    all_coefs(*coef_refs).wait_recv()
    totals[place.chan] = coef_in[...].sum(axis=0)
    total_refs = (totals, total_ss, total_rs, place)
    loop(1, N_CHAN, lambda n: total_copy(*total_refs, (place.chan + n) % N_CHAN, place.chan).start())
    samples.all_copies()[2].wait_recv()

    def coarse_diff(chan):
        coarse.diff[...] = samples.diff_in[rows_of(chan, GROUP)].astype(F32)

    send_diffs(coarse, place, coarse_diff)
    finish_update(coarse, place)
    loop(1, N_CHAN, lambda n: total_copy(*total_refs, place.chan, (place.chan + n) % N_CHAN).wait_recv())
    total = totals[...].sum(axis=0)
    for index, layer in enumerate(layers):
        finish_logit(layer, place, total[index : index + 1, 0:BANKS])
    finish_update(fine, place)
    finish_delta(coarse, place)
    send_diffs(fine, place, functools.partial(diff_of, fine, place))
    finish_delta(fine, place)

    for layer in layers:
        for kind in range(4):
            bank_copy(layer, place, kind).wait_send()
        for kind in range(6):
            part_copy(layer, place, kind).wait_send()
        for kind in range(3):
            diff_copy(layer, place, kind).wait_send()
    all_grads(fine, place).wait_send()
    many_kernels(fine, place, 0, 0, N_XY - 1).wait_send()
    for copy in samples.all_copies():
        copy.wait_send()
    all_coefs(*coef_refs).wait_send()
    loop(1, N_CHAN, lambda n: total_copy(*total_refs, (place.chan + n) % N_CHAN, place.chan).wait_send())


def store(*refs):
    given, out, held, (in_sem, out_sem) = refs[:6], refs[6:12], refs[12:18], refs[18:]
    loads = [pltpu.make_async_copy(given[n], held[n], in_sem.at[n]) for n in range(6)]
    stores = [pltpu.make_async_copy(held[n], out[n], out_sem.at[n]) for n in range(6)]
    for copy in loads:
        copy.start()
    for first, second in zip(loads, stores):
        first.wait()
        second.start()
    for copy in stores:
        copy.wait()


def per_device(
    fine_inputs,
    fine_upstream,
    fine_bank,
    fine_coefs,
    coarse_inputs,
    coarse_upstream,
    coarse_bank,
    coarse_coefs,
):
    vmem = pl.BlockSpec(memory_space=pltpu.VMEM)
    hbm = pl.BlockSpec(memory_space=pltpu.HBM)
    out_shape = []
    for side in (FINE_SIDE, COARSE_SIDE):
        out_shape += [
            jax.ShapeDtypeStruct((side * side, GROUP), BF16),
            jax.ShapeDtypeStruct((BANKS, TAPS, OWN, GROUP), F32),
            jax.ShapeDtypeStruct((1, BANKS), F32),
        ]
    results = pl.pallas_call(
        kernel,
        out_shape=out_shape,
        in_specs=[hbm] * 8,
        out_specs=[vmem] * 6,
        scratch_shapes=layer_scratch(FINE_SIDE)
        + layer_scratch(COARSE_SIDE)
        + [
            pltpu.VMEM((N_XY, 8, GROUP), F32),
            pltpu.VMEM((N_XY, 8, GROUP), F32),
            pltpu.VMEM((N_CHAN, 8, GROUP), F32),
            pltpu.SemaphoreType.DMA((1,)),
            pltpu.SemaphoreType.DMA((1,)),
            pltpu.SemaphoreType.DMA((N_CHAN,)),
            pltpu.SemaphoreType.DMA((N_CHAN,)),
            pltpu.VMEM((N_XY, COARSE_SIDE * COARSE_SIDE, GROUP), BF16),
            pltpu.VMEM((CHANNELS, COARSE_SIDE * COARSE_SIDE), BF16),
            pltpu.VMEM((AT_ONCE, COARSE_SIDE * COARSE_SIDE + 2 * COARSE_SIDE, ROW3), BF16),
            pltpu.VMEM((CHANNELS, COARSE_SIDE * COARSE_SIDE), BF16),
            pltpu.VMEM((CHANNELS, COARSE_SIDE * COARSE_SIDE), BF16),
        ]
        + [pltpu.SemaphoreType.DMA((1,))] * 6,
        compiler_params=pltpu.CompilerParams(
            collective_id=0, has_side_effects=True, vmem_limit_bytes=62 * MIB
        ),
    )(
        fine_inputs.reshape(FINE_SIDE * FINE_SIDE, CHANNELS),
        fine_upstream.reshape(FINE_SIDE * FINE_SIDE, GROUP),
        fine_bank,
        fine_coefs.T,
        coarse_inputs.reshape(COARSE_SIDE * COARSE_SIDE, CHANNELS),
        coarse_upstream.reshape(COARSE_SIDE * COARSE_SIDE, GROUP),
        coarse_bank,
        coarse_coefs.T,
    )
    fine_delta, fine_update, fine_logit, coarse_delta, coarse_update, coarse_logit = pl.pallas_call(
        store,
        out_shape=out_shape,
        in_specs=[hbm] * 6,
        out_specs=[hbm] * 6,
        scratch_shapes=[pltpu.VMEM(out.shape, out.dtype) for out in out_shape]
        + [pltpu.SemaphoreType.DMA((6,)), pltpu.SemaphoreType.DMA((6,))],
        compiler_params=pltpu.CompilerParams(vmem_limit_bytes=62 * MIB),
    )(*results)
    return (
        fine_delta.reshape(1, FINE_SIDE, FINE_SIDE, GROUP),
        fine_update,
        fine_logit,
        coarse_delta.reshape(1, COARSE_SIDE, COARSE_SIDE, GROUP),
        coarse_update,
        coarse_logit,
    )


def solution(mesh):
    return jax.shard_map(
        per_device,
        mesh=mesh,
        in_specs=(
            P("batch", None, None, None),
            P("batch", None, None, "chan"),
            P(None, None, "batch", "chan"),
            P(),
            P("batch", None, None, None),
            P("batch", None, None, "chan"),
            P(None, None, "batch", "chan"),
            P(),
        ),
        out_specs=(
            P("batch", None, None, "chan"),
            P(None, None, "batch", "chan"),
            P("batch", None),
            P("batch", None, None, "chan"),
            P(None, None, "batch", "chan"),
            P("batch", None),
        ),
        check_vma=False,
    )
```

```python
import functools

import jax
import jax.numpy as jnp
from jax import lax
from jax.experimental import pallas as pl
from jax.experimental.pallas import tpu as pltpu
from jax.sharding import PartitionSpec as P

BANKS = 8
TAPS = 9
CHANNELS = 512
GROUP = 128
FINE_SIDE = 32
COARSE_SIDE = 16
STEP = 128
AT_ONCE = 4
SAMPLES = 64
N_XY = 16
N_Z = 4
N_CHAN = 4
ROWS = CHANNELS // N_XY
OWN = 8
WIDE = TAPS * GROUP
ROW3 = 3 * GROUP
BLOCK = BANKS * OWN
HALF = BLOCK // 2
BANK_ROWS = N_Z * BLOCK

MIB = 1024 * 1024
MESH = pl.DeviceIdType.MESH
HIGH = lax.Precision.HIGHEST
F32 = jnp.float32
BF16 = jnp.bfloat16


def iota(shape, axis):
    return lax.broadcasted_iota(jnp.int32, shape, axis)


def mm(a, b, contract, precision=None):
    dims = (((contract[0],), (contract[1],)), ((), ()))
    return lax.dot_general(a, b, dims, precision=precision, preferred_element_type=F32)


class Layer:
    def __init__(self, side, args, delta, update, logit, scratch):
        self.side, self.args = side, args
        self.delta, self.update, self.logit = delta, update, logit
        (
            self.inputs, self.upstream, self.bank, self.coefs, self.load_sem,
            self.shifts, self.flipped, self.spread, self.cross, self.banks, self.mix, self.back,
            self.grad_out, self.grad_in, self.kern_out, self.kern_in,
            self.part, self.part_out, self.part_in, self.relay, self.diff, self.diff_out, self.diff_in,
            self.bank_ss, self.bank_rs, self.grad_ss, self.grad_rs, self.kern_ss, self.kern_rs,
            self.part_ss, self.part_rs, self.diff_ss, self.diff_rs,
        ) = scratch


def layer_scratch(side):
    pixels = side * side
    diff = (pixels, GROUP) if side == FINE_SIDE else (GROUP, pixels)
    return [
        pltpu.VMEM((pixels, CHANNELS), BF16),
        pltpu.VMEM((pixels, GROUP), BF16),
        pltpu.VMEM((BANKS, TAPS, OWN, GROUP), BF16),
        pltpu.VMEM((BANKS, SAMPLES), F32),
        pltpu.SemaphoreType.DMA((4,)),
        pltpu.VMEM((pixels + 2 * side, ROW3), BF16),
        pltpu.VMEM((CHANNELS, pixels), BF16),
        pltpu.VMEM((N_XY, BANK_ROWS), F32),
        pltpu.VMEM((N_XY, BANK_ROWS), F32),
        pltpu.VMEM((BANK_ROWS, WIDE), BF16),
        pltpu.VMEM((2, CHANNELS, BANK_ROWS), BF16),
        pltpu.VMEM((2, BANK_ROWS, CHANNELS), BF16),
        pltpu.VMEM((CHANNELS, WIDE), BF16),
        pltpu.VMEM((CHANNELS, WIDE), BF16),
        pltpu.VMEM((CHANNELS, WIDE), BF16),
        pltpu.VMEM((CHANNELS, WIDE), BF16),
        pltpu.VMEM((N_Z, BLOCK, WIDE), F32),
        pltpu.VMEM((N_Z, BLOCK, WIDE), BF16),
        pltpu.VMEM((2, BLOCK, WIDE), BF16),
        pltpu.VMEM((2, HALF, WIDE), BF16),
        pltpu.VMEM(diff, F32),
        pltpu.VMEM((3, *diff), BF16),
        pltpu.VMEM((3, *diff), BF16),
    ] + [
        pltpu.SemaphoreType.DMA((n,))
        for n in (4, 4, 1, 1, 1, 4, 6, 6, 3, 3)
    ]


N_LAYER_SCRATCH = 33


class Place:
    def __init__(self):
        self.batch = lax.axis_index("batch")
        self.chan = lax.axis_index("chan")
        self.xy = self.batch // N_Z
        self.z = self.batch % N_Z
        self.sibling = self.chan + 1 - 2 * (self.chan % 2)
        self.across = (self.chan + 2) % N_CHAN

    def at_xy(self, xy):
        return (xy * N_Z + self.z, self.chan)

    def at_z(self, z):
        return (self.xy * N_Z + z, self.chan)

    def at_chan(self, chan):
        return (self.batch, chan)


def rows_of(index, count):
    return pl.ds(pl.multiple_of(index * count, count), count)


def bank_copy(layer, place, kind, received=False):
    step = N_Z - 1 if kind % 2 else 1
    origin = place.z if kind < 2 else (place.z + N_Z - step) % N_Z
    if received:
        origin = (origin + N_Z - step) % N_Z
    if kind < 2:
        rows = rows_of(origin, BLOCK)
    else:
        rows = rows_of(2 * origin + kind - 2, HALF)
    return pltpu.make_async_remote_copy(
        src_ref=layer.banks.at[rows],
        dst_ref=layer.banks.at[rows],
        send_sem=layer.bank_ss.at[kind],
        recv_sem=layer.bank_rs.at[kind],
        device_id=place.at_z((place.z + step) % N_Z),
        device_id_type=MESH,
    )


def grad_copy(layer, place, xy_to):
    return pltpu.make_async_remote_copy(
        src_ref=layer.grad_out.at[rows_of(xy_to, ROWS)],
        dst_ref=layer.grad_in.at[rows_of(place.xy, ROWS)],
        send_sem=layer.grad_ss.at[0],
        recv_sem=layer.grad_rs.at[0],
        device_id=place.at_xy(xy_to),
        device_id_type=MESH,
    )


def all_grads(layer, place):
    rows = pl.ds(0, (N_XY - 1) * ROWS)
    return pltpu.make_async_remote_copy(
        src_ref=layer.grad_out.at[rows],
        dst_ref=layer.grad_in.at[rows],
        send_sem=layer.grad_ss.at[0],
        recv_sem=layer.grad_rs.at[0],
        device_id=place.at_xy((place.xy + 1) % N_XY),
        device_id_type=MESH,
    )


def kern_copy(layer, place, xy_to):
    return pltpu.make_async_remote_copy(
        src_ref=layer.kern_out.at[rows_of(xy_to, ROWS)],
        dst_ref=layer.kern_in.at[rows_of(place.xy, ROWS)],
        send_sem=layer.kern_ss.at[0],
        recv_sem=layer.kern_rs.at[place.xy // 4],
        device_id=place.at_xy(xy_to),
        device_id_type=MESH,
    )


def many_kernels(layer, place, y, first, blocks):
    rows = pl.ds(pl.multiple_of(first * ROWS, ROWS), blocks * ROWS)
    return pltpu.make_async_remote_copy(
        src_ref=layer.kern_out.at[rows],
        dst_ref=layer.kern_in.at[rows],
        send_sem=layer.kern_ss.at[0],
        recv_sem=layer.kern_rs.at[y],
        device_id=place.at_xy((place.xy + 1) % N_XY),
        device_id_type=MESH,
    )


def part_copy(layer, place, kind):
    to = (place.z + (1 if kind in (0, 2, 3) else N_Z - 1)) % N_Z
    target = (place.z + 2) % N_Z if kind < 2 else to
    half = (0, 1, 1, 0, 0, 1)[kind]
    rows = pl.ds(half * HALF, HALF)
    if kind < 2:
        landing = layer.relay.at[kind]
    else:
        landing = layer.part_in.at[0 if kind < 4 else 1, rows]
    return pltpu.make_async_remote_copy(
        src_ref=layer.part_out.at[target, rows],
        dst_ref=landing,
        send_sem=layer.part_ss.at[kind],
        recv_sem=layer.part_rs.at[kind],
        device_id=place.at_z(to),
        device_id_type=MESH,
    )


def diff_copy(layer, place, kind):
    return pltpu.make_async_remote_copy(
        src_ref=layer.diff_out.at[kind],
        dst_ref=layer.diff_in.at[kind],
        send_sem=layer.diff_ss.at[kind],
        recv_sem=layer.diff_rs.at[kind],
        device_id=place.at_chan(place.across if kind == 1 else place.sibling),
        device_id_type=MESH,
    )


def coef_copy(out_ref, in_ref, send_sem, recv_sem, place, xy_to):
    return pltpu.make_async_remote_copy(
        src_ref=out_ref.at[xy_to],
        dst_ref=in_ref.at[place.xy],
        send_sem=send_sem.at[0],
        recv_sem=recv_sem.at[0],
        device_id=place.at_xy(xy_to),
        device_id_type=MESH,
    )


def all_coefs(out_ref, in_ref, send_sem, recv_sem, place):
    return pltpu.make_async_remote_copy(
        src_ref=out_ref.at[0 : N_XY - 1],
        dst_ref=in_ref.at[0 : N_XY - 1],
        send_sem=send_sem.at[0],
        recv_sem=recv_sem.at[0],
        device_id=place.at_xy((place.xy + 1) % N_XY),
        device_id_type=MESH,
    )


def total_copy(ref, send_sem, recv_sem, place, chan_to, chan_from):
    return pltpu.make_async_remote_copy(
        src_ref=ref.at[chan_from],
        dst_ref=ref.at[chan_from],
        send_sem=send_sem.at[chan_to],
        recv_sem=recv_sem.at[chan_from],
        device_id=place.at_chan(chan_to),
        device_id_type=MESH,
    )


def loop(low, high, body):
    lax.fori_loop(low, high, lambda n, carry: (body(n), carry)[1], 0)


INPUTS, UPSTREAM, BANK, COEFS = range(4)


def load(layer, which):
    held = (layer.inputs, layer.upstream, layer.bank, layer.coefs)[which]
    return pltpu.make_async_copy(layer.args[which], held, layer.load_sem.at[which])


def arrange_bank(layer, place):
    load(layer, BANK).wait()

    def move(tap):
        rows = layer.bank[:, tap].astype(F32).reshape(BLOCK, GROUP).astype(BF16)
        layer.banks[rows_of(place.z, BLOCK), rows_of(tap, GROUP)] = rows

    loop(0, TAPS, move)


def clear_edges(shifts, side):
    zeros = jnp.zeros((side, ROW3), BF16)
    shifts[0:side] = zeros
    shifts[shifts.shape[0] - side : shifts.shape[0]] = zeros


def shift_rows(upstream, shifts, side, n):
    column = iota((STEP, GROUP), 0) & (side - 1)
    up = upstream[rows_of(n, STEP)].astype(F32)
    after = jnp.where(column < side - 1, pltpu.roll(up, STEP - 1, 0), 0.0)
    before = jnp.where(column > 0, pltpu.roll(up, 1, 0), 0.0)
    rows = pl.ds(pl.multiple_of(n * STEP + side, side), STEP)
    for index, value in enumerate((after, up, before)):
        shifts[rows, index * GROUP : (index + 1) * GROUP] = value.astype(BF16)


def shift_upstream(layer):
    load(layer, UPSTREAM).wait()
    clear_edges(layer.shifts, layer.side)
    loop(0, layer.side * layer.side // STEP, lambda n: shift_rows(layer.upstream, layer.shifts, layer.side, n))


def window(layer, row_shift, first, count):
    start = pl.multiple_of((2 - row_shift) * layer.side + first, layer.side)
    return layer.shifts[pl.ds(start, count)]


def split(value, ref, rows):
    hi = value.astype(BF16)
    ref[0, rows] = hi
    ref[1, rows] = (value - hi.astype(F32)).astype(BF16)


def spread_coefs(layer, place):
    load(layer, COEFS).wait()
    chosen = iota((SAMPLES, N_XY), 0) == iota((SAMPLES, N_XY), 1) * N_Z + place.z
    own = mm(layer.coefs[...], chosen.astype(F32), (1, 0), HIGH)
    col = iota((BANKS, BANK_ROWS), 1)
    wide = ((col // OWN) % BANKS == iota((BANKS, BANK_ROWS), 0)).astype(F32)
    layer.spread[...] = mm(own, wide, (0, 0), HIGH)
    same = diagonal(ROWS)

    def sample(n):
        row = jnp.broadcast_to(layer.spread[pl.ds(n, 1), :], (ROWS, BANK_ROWS))
        split(jnp.where(same, row, 0.0), layer.mix, rows_of(n, ROWS))

    loop(0, N_XY, sample)
    col = iota((N_XY, CHANNELS), 1)
    tall = mm(own, (col // ROWS == iota((N_XY, CHANNELS), 0)).astype(F32), (1, 0), HIGH)
    tall = jnp.broadcast_to(tall[:, None, :], (BANKS, OWN, CHANNELS)).reshape(BLOCK, CHANNELS)
    row, col = iota((BLOCK, CHANNELS), 0), iota((BLOCK, CHANNELS), 1)

    def block(n):
        same = n * OWN + row % OWN == col % ROWS
        split(jnp.where(same, tall, 0.0), layer.back, rows_of(n, BLOCK))

    loop(0, N_Z, block)


def diagonal(rows):
    shape = (rows, BANK_ROWS)
    row, col = iota(shape, 0), iota(shape, 1)
    return row % ROWS == (col // BLOCK) * OWN + col % OWN


AROUND = (
    (1, 0), (0, 1), (3, 0), (0, 3), (1, 1), (3, 3), (2, 0), (0, 2),
    (1, 3), (3, 1), (2, 1), (2, 3), (1, 2), (3, 2), (2, 2),
)


def send_rows(place, copy):
    y, x = place.xy // 4, place.xy % 4
    for step_x, step_y in AROUND:
        copy((y + step_y) % 4 * 4 + (x + step_x) % 4).start()


def flip_inputs(layer):
    load(layer, INPUTS).wait()

    def flip(n):
        layer.flipped[rows_of(n, GROUP)] = layer.inputs[:, rows_of(n, GROUP)].T

    loop(0, CHANNELS // GROUP, flip)


def send_grads(layer, place):
    flip_inputs(layer)
    pixels = layer.side * layer.side

    def chunk(n):
        row_shift, part = n // 2, rows_of(n % 2, 2 * GROUP)
        grad = mm(layer.flipped[part], window(layer, row_shift, 0, pixels), (1, 0)) * (1.0 / layer.side)
        layer.grad_out[part, rows_of(row_shift, ROW3)] = grad.astype(BF16)

    loop(0, 6, chunk)
    send_rows(place, functools.partial(grad_copy, layer, place))
    own = rows_of(place.xy, ROWS)
    layer.grad_in[own, :] = layer.grad_out[own, :]


def forward_bank(layer, place):
    for kind in (0, 1):
        bank_copy(layer, place, kind, received=True).wait_recv()
        bank_copy(layer, place, kind + 2).start()


def mix_kernels(layer, place):
    for kind in (2, 3):
        bank_copy(layer, place, kind, received=True).wait_recv()

    def chunk(n):
        cols, part = rows_of(n // 2, ROW3), rows_of(n % 2, 2 * GROUP)
        banks = layer.banks[:, cols]
        mixed = mm(layer.mix[0, part], banks, (1, 0)) + mm(layer.mix[1, part], banks, (1, 0))
        layer.kern_out[part, cols] = mixed.astype(BF16)

    loop(0, 6, chunk)


def send_kernels(layer, place):
    mix_kernels(layer, place)
    send_rows(place, functools.partial(kern_copy, layer, place))
    own = rows_of(place.xy, ROWS)
    layer.kern_in[own, :] = layer.kern_out[own, :]


class Samples:
    def __init__(self, layer, place, scratch):
        self.layer, self.place = layer, place
        (
            self.upstream, self.inputs, self.shifts, self.diff_out, self.diff_in,
            self.up_ss, self.up_rs, self.in_ss, self.in_rs, self.diff_ss, self.diff_rs,
        ) = scratch

    def copy(self, source, target, send_sem, recv_sem, to):
        return pltpu.make_async_remote_copy(
            src_ref=source,
            dst_ref=target,
            send_sem=send_sem.at[0],
            recv_sem=recv_sem.at[0],
            device_id=self.place.at_xy(to),
            device_id_type=MESH,
        )

    def up_copy(self, to):
        return self.copy(self.layer.upstream, self.upstream.at[self.place.xy], self.up_ss, self.up_rs, to)

    def in_copy(self, to):
        rows, here = rows_of(to, ROWS), rows_of(self.place.xy, ROWS)
        return self.copy(self.layer.flipped.at[rows], self.inputs.at[here], self.in_ss, self.in_rs, to)

    def diff_copy(self, to):
        rows, here = rows_of(to, ROWS), rows_of(self.place.xy, ROWS)
        return self.copy(self.diff_out.at[rows], self.diff_in.at[here], self.diff_ss, self.diff_rs, to)

    def all_copies(self, which):
        some, rows = pl.ds(0, N_XY - 1), pl.ds(0, (N_XY - 1) * ROWS)
        refs = (
            (self.upstream.at[some], self.upstream.at[some], self.up_ss, self.up_rs),
            (self.layer.flipped.at[rows], self.inputs.at[rows], self.in_ss, self.in_rs),
            (self.diff_out.at[rows], self.diff_in.at[rows], self.diff_ss, self.diff_rs),
        )[which]
        return self.copy(*refs, (self.place.xy + 1) % N_XY)

    def send(self):
        place, own = self.place, rows_of(self.place.xy, ROWS)
        load(self.layer, UPSTREAM).wait()
        send_rows(place, self.up_copy)
        flip_inputs(self.layer)
        send_rows(place, self.in_copy)
        self.upstream[place.xy] = self.layer.upstream[...]
        self.inputs[own] = self.layer.flipped[own]

    def window(self, sample, row_shift):
        side = self.layer.side
        start = (2 - row_shift) * side
        return self.shifts[sample, start : start + side * side]

    def grads(self):
        layer, side = self.layer, self.layer.side
        self.all_copies(0).wait_recv()
        self.all_copies(1).wait_recv()

        def some(n):
            picked = [n * AT_ONCE + at for at in range(AT_ONCE)]
            for sample in picked:
                clear_edges(self.shifts.at[sample], side)
                for part in range(side * side // STEP):
                    shift_rows(self.upstream.at[sample], self.shifts.at[sample], side, part)
            for sample in picked:
                rows = rows_of(sample, ROWS)
                for row_shift in range(3):
                    grad = mm(self.inputs[rows], self.window(sample, row_shift), (1, 0)) * (1.0 / side)
                    layer.grad_in[rows, row_shift * ROW3 : (row_shift + 1) * ROW3] = grad.astype(BF16)

        loop(0, N_XY // AT_ONCE, some)

    def send_diffs(self):
        def some(n):
            for at in range(AT_ONCE):
                sample = n * AT_ONCE + at
                rows, diff = rows_of(sample, ROWS), None
                for row_shift in range(3):
                    cols = slice(row_shift * ROW3, (row_shift + 1) * ROW3)
                    term = mm(self.layer.kern_out[rows, cols], self.window(sample, row_shift), (1, 1))
                    diff = term if diff is None else diff + term
                self.diff_out[rows] = diff.astype(BF16)

        loop(0, N_XY // AT_ONCE, some)
        send_rows(self.place, self.diff_copy)
        own = rows_of(self.place.xy, ROWS)
        self.diff_in[own] = self.diff_out[own]


def send_parts(layer, place):
    def some(n):
        cols = rows_of(n, ROW3)
        grads = layer.grad_in[:, cols]
        total = mm(layer.back[0], grads, (1, 0)) + mm(layer.back[1], grads, (1, 0))
        total = total.reshape(N_Z, BLOCK, ROW3)
        layer.part[:, :, cols] = total
        layer.part_out[:, :, cols] = total.astype(BF16)

    loop(0, 3, some)
    for kind in (0, 1, 2, 4):
        part_copy(layer, place, kind).start()


def relay_parts(layer, place):
    for kind, half in ((0, 0), (1, 1)):
        part_copy(layer, place, kind).wait_recv()
        target = (place.z + (1 if kind == 0 else N_Z - 1)) % N_Z
        rows = slice(half * HALF, (half + 1) * HALF)
        total = layer.part[target, rows] + layer.relay[kind].astype(F32)
        layer.part_out[target, rows] = total.astype(BF16)
        part_copy(layer, place, 3 if kind == 0 else 5).start()


def coef_sums(layer):
    same = diagonal(STEP)

    def some(n):
        cross = mm(layer.grad_in[rows_of(n, STEP)], layer.banks[...], (1, 1))
        cross = jnp.where(same, cross, 0.0).reshape(STEP // ROWS, ROWS, BANK_ROWS).sum(axis=1)
        for sample in range(STEP // ROWS):
            layer.cross[pl.ds(n * (STEP // ROWS) + sample, 1), :] = cross[sample : sample + 1]

    loop(0, CHANNELS // STEP, some)
    row = iota((BANK_ROWS, GROUP), 0)
    pick = ((row // OWN) % BANKS == iota((BANK_ROWS, GROUP), 1)).astype(F32)
    return mm(layer.cross[...], pick, (1, 0), HIGH)


def diff_of(layer, place, chan):
    y, my_y = chan, place.xy // 4

    @pl.when(y != my_y)
    def _():
        many_kernels(layer, place, y, y * 4, 4).wait_recv()

    @pl.when(y == my_y)
    def _():
        many_kernels(layer, place, y, y * 4, 3).wait_recv()

    part, size = rows_of(chan, GROUP), 2 * STEP

    def some(n):
        diff = mm(window(layer, 0, n * size, size), layer.kern_in[part, 0:ROW3], (1, 1))
        for row_shift in (1, 2):
            cols = slice(row_shift * ROW3, (row_shift + 1) * ROW3)
            diff = diff + mm(window(layer, row_shift, n * size, size), layer.kern_in[part, cols], (1, 1))
        layer.diff[rows_of(n, size)] = diff

    loop(0, layer.side * layer.side // size, some)


def send_diffs(layer, place, diff_of):
    def target(n):
        base = (place.chan + 2 * (1 - n // 2)) % N_CHAN
        diff_of(base + (1 - n % 2) * (1 - 2 * (place.chan % 2)))

        @pl.when(n == 0)
        def _():
            layer.diff_out[0] = layer.diff[...].astype(BF16)
            diff_copy(layer, place, 0).start()

        @pl.when(n == 1)
        def _():
            diff_copy(layer, place, 0).wait_recv()
            layer.diff_out[1] = (layer.diff[...] + layer.diff_in[0].astype(F32)).astype(BF16)
            diff_copy(layer, place, 1).start()

        @pl.when(n == 2)
        def _():
            layer.diff_out[2] = layer.diff[...].astype(BF16)
            diff_copy(layer, place, 2).start()

    loop(0, N_CHAN, target)


def finish_update(layer, place):
    for kind in (2, 3, 4, 5):
        part_copy(layer, place, kind).wait_recv()
    total = layer.part[place.z] + layer.part_in[0].astype(F32) + layer.part_in[1].astype(F32)
    for tap in range(TAPS):
        cols = total[:, tap * GROUP : (tap + 1) * GROUP]
        layer.update[:, tap] = cols.reshape(BANKS, OWN, GROUP)


def finish_delta(layer, place):
    total = layer.diff[...]
    for kind in (2, 1):
        diff_copy(layer, place, kind).wait_recv()
        total = total + layer.diff_in[kind].astype(F32)
    layer.delta[...] = (total if layer.side == FINE_SIDE else total.T).astype(BF16)


def finish_logit(layer, place, total):
    chosen = (iota((1, SAMPLES), 1) == place.batch).astype(F32)
    coefs = mm(chosen, layer.coefs[...], (1, 1), HIGH)
    layer.logit[...] = coefs * (total - jnp.sum(coefs * total, axis=1, keepdims=True))


def kernel(*refs):
    args, outs, scratch = refs[:8], refs[8:14], refs[14:]
    fine = Layer(FINE_SIDE, args[:4], *outs[:3], scratch[:N_LAYER_SCRATCH])
    coarse = Layer(COARSE_SIDE, args[4:], *outs[3:], scratch[N_LAYER_SCRATCH : 2 * N_LAYER_SCRATCH])
    coef_out, coef_in, totals, coef_ss, coef_rs, total_ss, total_rs, *rest = scratch[2 * N_LAYER_SCRATCH :]
    layers = (fine, coarse)
    place = Place()
    samples = Samples(coarse, place, rest)

    for which in (BANK, UPSTREAM, INPUTS, COEFS):
        for layer in layers:
            load(layer, which).start()
    barrier = pltpu.get_barrier_semaphore()

    def greet(device):
        pl.semaphore_signal(barrier, inc=1, device_id=device, device_id_type=MESH)

    loop(1, N_XY, lambda n: greet(place.at_xy((place.xy + n) % N_XY)))
    for step in (1, N_Z - 1):
        greet(place.at_z((place.z + step) % N_Z))
    loop(1, N_CHAN, lambda n: greet(place.at_chan((place.chan + n) % N_CHAN)))
    for layer in layers:
        arrange_bank(layer, place)
    shift_upstream(fine)
    pl.semaphore_wait(barrier, N_XY + N_CHAN)

    for layer in layers:
        for kind in (0, 1):
            bank_copy(layer, place, kind).start()
    samples.send()
    send_grads(fine, place)
    forward_bank(fine, place)
    for layer in layers:
        spread_coefs(layer, place)
    forward_bank(coarse, place)
    send_kernels(fine, place)
    samples.grads()
    send_parts(coarse, place)
    mix_kernels(coarse, place)
    samples.send_diffs()
    relay_parts(coarse, place)
    coarse_sums = coef_sums(coarse)
    all_grads(fine, place).wait_recv()
    send_parts(fine, place)
    fine_sums = coef_sums(fine)
    shape = (N_XY, 8, GROUP)
    wide_sums = [jnp.broadcast_to(sums[:, None, :], shape) for sums in (fine_sums, coarse_sums)]
    coef_out[...] = jnp.where(iota(shape, 1) == 0, *wide_sums)
    coef_refs = (coef_out, coef_in, coef_ss, coef_rs, place)
    loop(1, N_XY, lambda n: coef_copy(*coef_refs, (place.xy + n) % N_XY).start())
    coef_in[place.xy] = coef_out[place.xy]
    samples.all_copies(2).wait_recv()

    def coarse_diff(chan):
        coarse.diff[...] = samples.diff_in[rows_of(chan, GROUP)].astype(F32)

    send_diffs(coarse, place, coarse_diff)
    relay_parts(fine, place)
    all_coefs(*coef_refs).wait_recv()
    totals[place.chan] = coef_in[...].sum(axis=0)
    total_refs = (totals, total_ss, total_rs, place)
    loop(1, N_CHAN, lambda n: total_copy(*total_refs, (place.chan + n) % N_CHAN, place.chan).start())
    send_diffs(fine, place, functools.partial(diff_of, fine, place))
    finish_update(coarse, place)
    finish_delta(coarse, place)
    loop(1, N_CHAN, lambda n: total_copy(*total_refs, place.chan, (place.chan + n) % N_CHAN).wait_recv())
    total = totals[...].sum(axis=0)
    for index, layer in enumerate(layers):
        finish_logit(layer, place, total[index : index + 1, 0:BANKS])
    finish_update(fine, place)
    finish_delta(fine, place)

    for layer in layers:
        for kind in range(4):
            bank_copy(layer, place, kind).wait_send()
        for kind in range(6):
            part_copy(layer, place, kind).wait_send()
        for kind in range(3):
            diff_copy(layer, place, kind).wait_send()
    all_grads(fine, place).wait_send()
    many_kernels(fine, place, 0, 0, N_XY - 1).wait_send()
    for which in range(3):
        samples.all_copies(which).wait_send()
    all_coefs(*coef_refs).wait_send()
    loop(1, N_CHAN, lambda n: total_copy(*total_refs, (place.chan + n) % N_CHAN, place.chan).wait_send())


def store(*refs):
    given, out, held, (in_sem, out_sem) = refs[:6], refs[6:12], refs[12:18], refs[18:]
    loads = [pltpu.make_async_copy(given[n], held[n], in_sem.at[n]) for n in range(6)]
    stores = [pltpu.make_async_copy(held[n], out[n], out_sem.at[n]) for n in range(6)]
    for copy in loads:
        copy.start()
    for first, second in zip(loads, stores):
        first.wait()
        second.start()
    for copy in stores:
        copy.wait()


def per_device(
    fine_inputs,
    fine_upstream,
    fine_bank,
    fine_coefs,
    coarse_inputs,
    coarse_upstream,
    coarse_bank,
    coarse_coefs,
):
    vmem = pl.BlockSpec(memory_space=pltpu.VMEM)
    hbm = pl.BlockSpec(memory_space=pltpu.HBM)
    out_shape = []
    for side in (FINE_SIDE, COARSE_SIDE):
        out_shape += [
            jax.ShapeDtypeStruct((side * side, GROUP), BF16),
            jax.ShapeDtypeStruct((BANKS, TAPS, OWN, GROUP), F32),
            jax.ShapeDtypeStruct((1, BANKS), F32),
        ]
    results = pl.pallas_call(
        kernel,
        out_shape=out_shape,
        in_specs=[hbm] * 8,
        out_specs=[vmem] * 6,
        scratch_shapes=layer_scratch(FINE_SIDE)
        + layer_scratch(COARSE_SIDE)
        + [
            pltpu.VMEM((N_XY, 8, GROUP), F32),
            pltpu.VMEM((N_XY, 8, GROUP), F32),
            pltpu.VMEM((N_CHAN, 8, GROUP), F32),
            pltpu.SemaphoreType.DMA((1,)),
            pltpu.SemaphoreType.DMA((1,)),
            pltpu.SemaphoreType.DMA((N_CHAN,)),
            pltpu.SemaphoreType.DMA((N_CHAN,)),
            pltpu.VMEM((N_XY, COARSE_SIDE * COARSE_SIDE, GROUP), BF16),
            pltpu.VMEM((CHANNELS, COARSE_SIDE * COARSE_SIDE), BF16),
            pltpu.VMEM((N_XY, COARSE_SIDE * COARSE_SIDE + 2 * COARSE_SIDE, ROW3), BF16),
            pltpu.VMEM((CHANNELS, COARSE_SIDE * COARSE_SIDE), BF16),
            pltpu.VMEM((CHANNELS, COARSE_SIDE * COARSE_SIDE), BF16),
        ]
        + [pltpu.SemaphoreType.DMA((1,))] * 6,
        compiler_params=pltpu.CompilerParams(
            collective_id=0, has_side_effects=True, vmem_limit_bytes=62 * MIB
        ),
    )(
        fine_inputs.reshape(FINE_SIDE * FINE_SIDE, CHANNELS),
        fine_upstream.reshape(FINE_SIDE * FINE_SIDE, GROUP),
        fine_bank,
        fine_coefs.T,
        coarse_inputs.reshape(COARSE_SIDE * COARSE_SIDE, CHANNELS),
        coarse_upstream.reshape(COARSE_SIDE * COARSE_SIDE, GROUP),
        coarse_bank,
        coarse_coefs.T,
    )
    fine_delta, fine_update, fine_logit, coarse_delta, coarse_update, coarse_logit = pl.pallas_call(
        store,
        out_shape=out_shape,
        in_specs=[hbm] * 6,
        out_specs=[hbm] * 6,
        scratch_shapes=[pltpu.VMEM(out.shape, out.dtype) for out in out_shape]
        + [pltpu.SemaphoreType.DMA((6,)), pltpu.SemaphoreType.DMA((6,))],
        compiler_params=pltpu.CompilerParams(vmem_limit_bytes=62 * MIB),
    )(*results)
    return (
        fine_delta.reshape(1, FINE_SIDE, FINE_SIDE, GROUP),
        fine_update,
        fine_logit,
        coarse_delta.reshape(1, COARSE_SIDE, COARSE_SIDE, GROUP),
        coarse_update,
        coarse_logit,
    )


def solution(mesh):
    return jax.shard_map(
        per_device,
        mesh=mesh,
        in_specs=(
            P("batch", None, None, None),
            P("batch", None, None, "chan"),
            P(None, None, "batch", "chan"),
            P(),
            P("batch", None, None, None),
            P("batch", None, None, "chan"),
            P(None, None, "batch", "chan"),
            P(),
        ),
        out_specs=(
            P("batch", None, None, "chan"),
            P(None, None, "batch", "chan"),
            P("batch", None),
            P("batch", None, None, "chan"),
            P(None, None, "batch", "chan"),
            P("batch", None),
        ),
        check_vma=False,
    )
```

```python
import functools

import jax
import jax.numpy as jnp
from jax import lax
from jax.experimental import pallas as pl
from jax.experimental.pallas import tpu as pltpu
from jax.sharding import PartitionSpec as P

BANKS = 8
TAPS = 9
CHANNELS = 512
GROUP = 128
FINE_SIDE = 32
COARSE_SIDE = 16
STEP = 128
AT_ONCE = 4
SAMPLES = 64
N_XY = 16
N_Z = 4
N_CHAN = 4
ROWS = CHANNELS // N_XY
OWN = 8
WIDE = TAPS * GROUP
ROW3 = 3 * GROUP
BLOCK = BANKS * OWN
HALF = BLOCK // 2
BANK_ROWS = N_Z * BLOCK

MIB = 1024 * 1024
MESH = pl.DeviceIdType.MESH
HIGH = lax.Precision.HIGHEST
F32 = jnp.float32
BF16 = jnp.bfloat16


def iota(shape, axis):
    return lax.broadcasted_iota(jnp.int32, shape, axis)


def mm(a, b, contract, precision=None):
    dims = (((contract[0],), (contract[1],)), ((), ()))
    return lax.dot_general(a, b, dims, precision=precision, preferred_element_type=F32)


class Layer:
    def __init__(self, side, args, delta, update, logit, scratch):
        self.side, self.args = side, args
        self.delta, self.update, self.logit = delta, update, logit
        (
            self.inputs, self.upstream, self.bank, self.coefs, self.load_sem,
            self.shifts, self.flipped, self.spread, self.cross, self.banks, self.mix, self.back,
            self.grad_out, self.grad_in, self.kern_out, self.kern_in,
            self.part, self.part_out, self.part_in, self.relay, self.diff, self.diff_out, self.diff_in,
            self.bank_ss, self.bank_rs, self.grad_ss, self.grad_rs, self.kern_ss, self.kern_rs,
            self.part_ss, self.part_rs, self.diff_ss, self.diff_rs,
        ) = scratch


def layer_scratch(side):
    pixels = side * side
    diff = (pixels, GROUP) if side == FINE_SIDE else (GROUP, pixels)
    return [
        pltpu.VMEM((pixels, CHANNELS), BF16),
        pltpu.VMEM((pixels, GROUP), BF16),
        pltpu.VMEM((BANKS, TAPS, OWN, GROUP), BF16),
        pltpu.VMEM((BANKS, SAMPLES), F32),
        pltpu.SemaphoreType.DMA((4,)),
        pltpu.VMEM((pixels + 2 * side, ROW3), BF16),
        pltpu.VMEM((CHANNELS, pixels), BF16),
        pltpu.VMEM((N_XY, BANK_ROWS), F32),
        pltpu.VMEM((N_XY, BANK_ROWS), F32),
        pltpu.VMEM((BANK_ROWS, WIDE), BF16),
        pltpu.VMEM((2, CHANNELS, BANK_ROWS), BF16),
        pltpu.VMEM((2, BANK_ROWS, CHANNELS), BF16),
        pltpu.VMEM((CHANNELS, WIDE), BF16),
        pltpu.VMEM((CHANNELS, WIDE), BF16),
        pltpu.VMEM((CHANNELS, WIDE), BF16),
        pltpu.VMEM((CHANNELS, WIDE), BF16),
        pltpu.VMEM((N_Z, BLOCK, WIDE), F32),
        pltpu.VMEM((N_Z, BLOCK, WIDE), BF16),
        pltpu.VMEM((2, BLOCK, WIDE), BF16),
        pltpu.VMEM((2, HALF, WIDE), BF16),
        pltpu.VMEM(diff, F32),
        pltpu.VMEM((3, *diff), BF16),
        pltpu.VMEM((3, *diff), BF16),
    ] + [
        pltpu.SemaphoreType.DMA((n,))
        for n in (4, 4, 1, 1, 1, 4, 6, 6, 3, 3)
    ]


N_LAYER_SCRATCH = 33


class Place:
    def __init__(self):
        self.batch = lax.axis_index("batch")
        self.chan = lax.axis_index("chan")
        self.xy = self.batch // N_Z
        self.z = self.batch % N_Z
        self.sibling = self.chan + 1 - 2 * (self.chan % 2)
        self.across = (self.chan + 2) % N_CHAN

    def at_xy(self, xy):
        return (xy * N_Z + self.z, self.chan)

    def at_z(self, z):
        return (self.xy * N_Z + z, self.chan)

    def at_chan(self, chan):
        return (self.batch, chan)


def rows_of(index, count):
    return pl.ds(pl.multiple_of(index * count, count), count)


def bank_copy(layer, place, kind, received=False):
    step = N_Z - 1 if kind % 2 else 1
    origin = place.z if kind < 2 else (place.z + N_Z - step) % N_Z
    if received:
        origin = (origin + N_Z - step) % N_Z
    if kind < 2:
        rows = rows_of(origin, BLOCK)
    else:
        rows = rows_of(2 * origin + kind - 2, HALF)
    return pltpu.make_async_remote_copy(
        src_ref=layer.banks.at[rows],
        dst_ref=layer.banks.at[rows],
        send_sem=layer.bank_ss.at[kind],
        recv_sem=layer.bank_rs.at[kind],
        device_id=place.at_z((place.z + step) % N_Z),
        device_id_type=MESH,
    )


def grad_copy(layer, place, xy_to):
    return pltpu.make_async_remote_copy(
        src_ref=layer.grad_out.at[rows_of(xy_to, ROWS)],
        dst_ref=layer.grad_in.at[rows_of(place.xy, ROWS)],
        send_sem=layer.grad_ss.at[0],
        recv_sem=layer.grad_rs.at[0],
        device_id=place.at_xy(xy_to),
        device_id_type=MESH,
    )


def all_grads(layer, place):
    rows = pl.ds(0, (N_XY - 1) * ROWS)
    return pltpu.make_async_remote_copy(
        src_ref=layer.grad_out.at[rows],
        dst_ref=layer.grad_in.at[rows],
        send_sem=layer.grad_ss.at[0],
        recv_sem=layer.grad_rs.at[0],
        device_id=place.at_xy((place.xy + 1) % N_XY),
        device_id_type=MESH,
    )


def kern_copy(layer, place, xy_to):
    return pltpu.make_async_remote_copy(
        src_ref=layer.kern_out.at[rows_of(xy_to, ROWS)],
        dst_ref=layer.kern_in.at[rows_of(place.xy, ROWS)],
        send_sem=layer.kern_ss.at[0],
        recv_sem=layer.kern_rs.at[place.xy // 4],
        device_id=place.at_xy(xy_to),
        device_id_type=MESH,
    )


def many_kernels(layer, place, y, first, blocks):
    rows = pl.ds(pl.multiple_of(first * ROWS, ROWS), blocks * ROWS)
    return pltpu.make_async_remote_copy(
        src_ref=layer.kern_out.at[rows],
        dst_ref=layer.kern_in.at[rows],
        send_sem=layer.kern_ss.at[0],
        recv_sem=layer.kern_rs.at[y],
        device_id=place.at_xy((place.xy + 1) % N_XY),
        device_id_type=MESH,
    )


def part_copy(layer, place, kind):
    to = (place.z + (1 if kind in (0, 2, 3) else N_Z - 1)) % N_Z
    target = (place.z + 2) % N_Z if kind < 2 else to
    half = (0, 1, 1, 0, 0, 1)[kind]
    rows = pl.ds(half * HALF, HALF)
    if kind < 2:
        landing = layer.relay.at[kind]
    else:
        landing = layer.part_in.at[0 if kind < 4 else 1, rows]
    return pltpu.make_async_remote_copy(
        src_ref=layer.part_out.at[target, rows],
        dst_ref=landing,
        send_sem=layer.part_ss.at[kind],
        recv_sem=layer.part_rs.at[kind],
        device_id=place.at_z(to),
        device_id_type=MESH,
    )


def diff_copy(layer, place, kind):
    return pltpu.make_async_remote_copy(
        src_ref=layer.diff_out.at[kind],
        dst_ref=layer.diff_in.at[kind],
        send_sem=layer.diff_ss.at[kind],
        recv_sem=layer.diff_rs.at[kind],
        device_id=place.at_chan(place.across if kind == 1 else place.sibling),
        device_id_type=MESH,
    )


def coef_copy(out_ref, in_ref, send_sem, recv_sem, place, xy_to):
    return pltpu.make_async_remote_copy(
        src_ref=out_ref.at[xy_to],
        dst_ref=in_ref.at[place.xy],
        send_sem=send_sem.at[0],
        recv_sem=recv_sem.at[0],
        device_id=place.at_xy(xy_to),
        device_id_type=MESH,
    )


def all_coefs(out_ref, in_ref, send_sem, recv_sem, place):
    return pltpu.make_async_remote_copy(
        src_ref=out_ref.at[0 : N_XY - 1],
        dst_ref=in_ref.at[0 : N_XY - 1],
        send_sem=send_sem.at[0],
        recv_sem=recv_sem.at[0],
        device_id=place.at_xy((place.xy + 1) % N_XY),
        device_id_type=MESH,
    )


def total_copy(ref, send_sem, recv_sem, place, chan_to, chan_from):
    return pltpu.make_async_remote_copy(
        src_ref=ref.at[chan_from],
        dst_ref=ref.at[chan_from],
        send_sem=send_sem.at[chan_to],
        recv_sem=recv_sem.at[chan_from],
        device_id=place.at_chan(chan_to),
        device_id_type=MESH,
    )


def loop(low, high, body):
    lax.fori_loop(low, high, lambda n, carry: (body(n), carry)[1], 0)


INPUTS, UPSTREAM, BANK, COEFS = range(4)


def load(layer, which):
    held = (layer.inputs, layer.upstream, layer.bank, layer.coefs)[which]
    return pltpu.make_async_copy(layer.args[which], held, layer.load_sem.at[which])


def arrange_bank(layer, place):
    load(layer, BANK).wait()

    def move(tap):
        rows = layer.bank[:, tap].astype(F32).reshape(BLOCK, GROUP).astype(BF16)
        layer.banks[rows_of(place.z, BLOCK), rows_of(tap, GROUP)] = rows

    loop(0, TAPS, move)


def clear_edges(shifts, side):
    zeros = jnp.zeros((side, ROW3), BF16)
    shifts[0:side] = zeros
    shifts[shifts.shape[0] - side : shifts.shape[0]] = zeros


def shift_rows(upstream, shifts, side, n):
    column = iota((STEP, GROUP), 0) & (side - 1)
    up = upstream[rows_of(n, STEP)].astype(F32)
    after = jnp.where(column < side - 1, pltpu.roll(up, STEP - 1, 0), 0.0)
    before = jnp.where(column > 0, pltpu.roll(up, 1, 0), 0.0)
    rows = pl.ds(pl.multiple_of(n * STEP + side, side), STEP)
    for index, value in enumerate((after, up, before)):
        shifts[rows, index * GROUP : (index + 1) * GROUP] = value.astype(BF16)


def shift_upstream(layer):
    load(layer, UPSTREAM).wait()
    clear_edges(layer.shifts, layer.side)
    loop(0, layer.side * layer.side // STEP, lambda n: shift_rows(layer.upstream, layer.shifts, layer.side, n))


def window(layer, row_shift, first, count):
    start = pl.multiple_of((2 - row_shift) * layer.side + first, layer.side)
    return layer.shifts[pl.ds(start, count)]


def split(value, ref, rows):
    hi = value.astype(BF16)
    ref[0, rows] = hi
    ref[1, rows] = (value - hi.astype(F32)).astype(BF16)


def spread_coefs(layer, place):
    load(layer, COEFS).wait()
    chosen = iota((SAMPLES, N_XY), 0) == iota((SAMPLES, N_XY), 1) * N_Z + place.z
    own = mm(layer.coefs[...], chosen.astype(F32), (1, 0), HIGH)
    col = iota((BANKS, BANK_ROWS), 1)
    wide = ((col // OWN) % BANKS == iota((BANKS, BANK_ROWS), 0)).astype(F32)
    layer.spread[...] = mm(own, wide, (0, 0), HIGH)
    same = diagonal(ROWS)

    def sample(n):
        row = jnp.broadcast_to(layer.spread[pl.ds(n, 1), :], (ROWS, BANK_ROWS))
        split(jnp.where(same, row, 0.0), layer.mix, rows_of(n, ROWS))

    loop(0, N_XY, sample)
    col = iota((N_XY, CHANNELS), 1)
    tall = mm(own, (col // ROWS == iota((N_XY, CHANNELS), 0)).astype(F32), (1, 0), HIGH)
    tall = jnp.broadcast_to(tall[:, None, :], (BANKS, OWN, CHANNELS)).reshape(BLOCK, CHANNELS)
    row, col = iota((BLOCK, CHANNELS), 0), iota((BLOCK, CHANNELS), 1)

    def block(n):
        same = n * OWN + row % OWN == col % ROWS
        split(jnp.where(same, tall, 0.0), layer.back, rows_of(n, BLOCK))

    loop(0, N_Z, block)


def diagonal(rows):
    shape = (rows, BANK_ROWS)
    row, col = iota(shape, 0), iota(shape, 1)
    return row % ROWS == (col // BLOCK) * OWN + col % OWN


AROUND = (
    (1, 0), (0, 1), (3, 0), (0, 3), (1, 1), (3, 3), (2, 0), (0, 2),
    (1, 3), (3, 1), (2, 1), (2, 3), (1, 2), (3, 2), (2, 2),
)


def send_rows(place, copy):
    y, x = place.xy // 4, place.xy % 4
    for step_x, step_y in AROUND:
        copy((y + step_y) % 4 * 4 + (x + step_x) % 4).start()


def flip_inputs(layer):
    load(layer, INPUTS).wait()

    def flip(n):
        layer.flipped[rows_of(n, GROUP)] = layer.inputs[:, rows_of(n, GROUP)].T

    loop(0, CHANNELS // GROUP, flip)


def send_grads(layer, place):
    flip_inputs(layer)
    pixels = layer.side * layer.side

    def chunk(n):
        row_shift, part = n // 2, rows_of(n % 2, 2 * GROUP)
        grad = mm(layer.flipped[part], window(layer, row_shift, 0, pixels), (1, 0)) * (1.0 / layer.side)
        layer.grad_out[part, rows_of(row_shift, ROW3)] = grad.astype(BF16)

    loop(0, 6, chunk)
    send_rows(place, functools.partial(grad_copy, layer, place))
    own = rows_of(place.xy, ROWS)
    layer.grad_in[own, :] = layer.grad_out[own, :]


def forward_bank(layer, place):
    for kind in (0, 1):
        bank_copy(layer, place, kind, received=True).wait_recv()
        bank_copy(layer, place, kind + 2).start()


def mix_kernels(layer, place):
    for kind in (2, 3):
        bank_copy(layer, place, kind, received=True).wait_recv()

    def chunk(n):
        cols, part = rows_of(n // 2, ROW3), rows_of(n % 2, 2 * GROUP)
        banks = layer.banks[:, cols]
        mixed = mm(layer.mix[0, part], banks, (1, 0)) + mm(layer.mix[1, part], banks, (1, 0))
        layer.kern_out[part, cols] = mixed.astype(BF16)

    loop(0, 6, chunk)


def send_kernels(layer, place):
    mix_kernels(layer, place)
    send_rows(place, functools.partial(kern_copy, layer, place))
    own = rows_of(place.xy, ROWS)
    layer.kern_in[own, :] = layer.kern_out[own, :]


class Samples:
    def __init__(self, layer, place, scratch):
        self.layer, self.place = layer, place
        (
            self.upstream, self.inputs, self.shifts, self.diff_out, self.diff_in,
            self.up_ss, self.up_rs, self.in_ss, self.in_rs, self.diff_ss, self.diff_rs,
        ) = scratch

    def copy(self, source, target, send_sem, recv_sem, to):
        return pltpu.make_async_remote_copy(
            src_ref=source,
            dst_ref=target,
            send_sem=send_sem.at[0],
            recv_sem=recv_sem.at[0],
            device_id=self.place.at_xy(to),
            device_id_type=MESH,
        )

    def up_copy(self, to):
        return self.copy(self.layer.upstream, self.upstream.at[self.place.xy], self.up_ss, self.up_rs, to)

    def in_copy(self, to):
        rows, here = rows_of(to, ROWS), rows_of(self.place.xy, ROWS)
        return self.copy(self.layer.flipped.at[rows], self.inputs.at[here], self.in_ss, self.in_rs, to)

    def diff_copy(self, to):
        rows, here = rows_of(to, ROWS), rows_of(self.place.xy, ROWS)
        return self.copy(self.diff_out.at[rows], self.diff_in.at[here], self.diff_ss, self.diff_rs, to)

    def all_copies(self, which):
        some, rows = pl.ds(0, N_XY - 1), pl.ds(0, (N_XY - 1) * ROWS)
        refs = (
            (self.upstream.at[some], self.upstream.at[some], self.up_ss, self.up_rs),
            (self.layer.flipped.at[rows], self.inputs.at[rows], self.in_ss, self.in_rs),
            (self.diff_out.at[rows], self.diff_in.at[rows], self.diff_ss, self.diff_rs),
        )[which]
        return self.copy(*refs, (self.place.xy + 1) % N_XY)

    def send(self):
        place, own = self.place, rows_of(self.place.xy, ROWS)
        load(self.layer, UPSTREAM).wait()
        send_rows(place, self.up_copy)
        flip_inputs(self.layer)
        send_rows(place, self.in_copy)
        self.upstream[place.xy] = self.layer.upstream[...]
        self.inputs[own] = self.layer.flipped[own]

    def window(self, sample, row_shift):
        side = self.layer.side
        start = (2 - row_shift) * side
        return self.shifts[sample, start : start + side * side]

    def grads(self):
        layer, side = self.layer, self.layer.side
        self.all_copies(0).wait_recv()
        self.all_copies(1).wait_recv()

        def some(n):
            picked = [n * AT_ONCE + at for at in range(AT_ONCE)]
            for sample in picked:
                clear_edges(self.shifts.at[sample], side)
                for part in range(side * side // STEP):
                    shift_rows(self.upstream.at[sample], self.shifts.at[sample], side, part)
            for sample in picked:
                rows = rows_of(sample, ROWS)
                for row_shift in range(3):
                    grad = mm(self.inputs[rows], self.window(sample, row_shift), (1, 0)) * (1.0 / side)
                    layer.grad_in[rows, row_shift * ROW3 : (row_shift + 1) * ROW3] = grad.astype(BF16)

        loop(0, N_XY // AT_ONCE, some)

    def send_diffs(self):
        def some(n):
            for at in range(AT_ONCE):
                sample = n * AT_ONCE + at
                rows, diff = rows_of(sample, ROWS), None
                for row_shift in range(3):
                    cols = slice(row_shift * ROW3, (row_shift + 1) * ROW3)
                    term = mm(self.layer.kern_out[rows, cols], self.window(sample, row_shift), (1, 1))
                    diff = term if diff is None else diff + term
                self.diff_out[rows] = diff.astype(BF16)

        loop(0, N_XY // AT_ONCE, some)
        send_rows(self.place, self.diff_copy)
        own = rows_of(self.place.xy, ROWS)
        self.diff_in[own] = self.diff_out[own]


def send_parts(layer, place):
    def some(n):
        cols = rows_of(n, ROW3)
        grads = layer.grad_in[:, cols]
        total = mm(layer.back[0], grads, (1, 0)) + mm(layer.back[1], grads, (1, 0))
        total = total.reshape(N_Z, BLOCK, ROW3)
        layer.part[:, :, cols] = total
        layer.part_out[:, :, cols] = total.astype(BF16)

    loop(0, 3, some)
    for kind in (0, 1, 2, 4):
        part_copy(layer, place, kind).start()


def relay_parts(layer, place):
    for kind, half in ((0, 0), (1, 1)):
        part_copy(layer, place, kind).wait_recv()
        target = (place.z + (1 if kind == 0 else N_Z - 1)) % N_Z
        rows = slice(half * HALF, (half + 1) * HALF)
        total = layer.part[target, rows] + layer.relay[kind].astype(F32)
        layer.part_out[target, rows] = total.astype(BF16)
        part_copy(layer, place, 3 if kind == 0 else 5).start()


def coef_sums(layer):
    same = diagonal(STEP)

    def some(n):
        cross = mm(layer.grad_in[rows_of(n, STEP)], layer.banks[...], (1, 1))
        cross = jnp.where(same, cross, 0.0).reshape(STEP // ROWS, ROWS, BANK_ROWS).sum(axis=1)
        for sample in range(STEP // ROWS):
            layer.cross[pl.ds(n * (STEP // ROWS) + sample, 1), :] = cross[sample : sample + 1]

    loop(0, CHANNELS // STEP, some)
    row = iota((BANK_ROWS, GROUP), 0)
    pick = ((row // OWN) % BANKS == iota((BANK_ROWS, GROUP), 1)).astype(F32)
    return mm(layer.cross[...], pick, (1, 0), HIGH)


def diff_of(layer, place, chan):
    y, my_y = chan, place.xy // 4

    @pl.when(y != my_y)
    def _():
        many_kernels(layer, place, y, y * 4, 4).wait_recv()

    @pl.when(y == my_y)
    def _():
        many_kernels(layer, place, y, y * 4, 3).wait_recv()

    part, size = rows_of(chan, GROUP), 2 * STEP

    def some(n):
        diff = mm(window(layer, 0, n * size, size), layer.kern_in[part, 0:ROW3], (1, 1))
        for row_shift in (1, 2):
            cols = slice(row_shift * ROW3, (row_shift + 1) * ROW3)
            diff = diff + mm(window(layer, row_shift, n * size, size), layer.kern_in[part, cols], (1, 1))
        layer.diff[rows_of(n, size)] = diff

    loop(0, layer.side * layer.side // size, some)


def send_diffs(layer, place, diff_of):
    def target(n):
        base = (place.chan + 2 * (1 - n // 2)) % N_CHAN
        diff_of(base + (1 - n % 2) * (1 - 2 * (place.chan % 2)))

        @pl.when(n == 0)
        def _():
            layer.diff_out[0] = layer.diff[...].astype(BF16)
            diff_copy(layer, place, 0).start()

        @pl.when(n == 1)
        def _():
            diff_copy(layer, place, 0).wait_recv()
            layer.diff_out[1] = (layer.diff[...] + layer.diff_in[0].astype(F32)).astype(BF16)
            diff_copy(layer, place, 1).start()

        @pl.when(n == 2)
        def _():
            layer.diff_out[2] = layer.diff[...].astype(BF16)
            diff_copy(layer, place, 2).start()

    loop(0, N_CHAN, target)


def finish_update(layer, place):
    for kind in (2, 3, 4, 5):
        part_copy(layer, place, kind).wait_recv()
    total = layer.part[place.z] + layer.part_in[0].astype(F32) + layer.part_in[1].astype(F32)
    for tap in range(TAPS):
        cols = total[:, tap * GROUP : (tap + 1) * GROUP]
        layer.update[:, tap] = cols.reshape(BANKS, OWN, GROUP)


def finish_delta(layer, place):
    total = layer.diff[...]
    for kind in (2, 1):
        diff_copy(layer, place, kind).wait_recv()
        total = total + layer.diff_in[kind].astype(F32)
    layer.delta[...] = (total if layer.side == FINE_SIDE else total.T).astype(BF16)


def finish_logit(layer, place, total):
    chosen = (iota((1, SAMPLES), 1) == place.batch).astype(F32)
    coefs = mm(chosen, layer.coefs[...], (1, 1), HIGH)
    layer.logit[...] = coefs * (total - jnp.sum(coefs * total, axis=1, keepdims=True))


def kernel(*refs):
    args, outs, scratch = refs[:8], refs[8:14], refs[14:]
    fine = Layer(FINE_SIDE, args[:4], *outs[:3], scratch[:N_LAYER_SCRATCH])
    coarse = Layer(COARSE_SIDE, args[4:], *outs[3:], scratch[N_LAYER_SCRATCH : 2 * N_LAYER_SCRATCH])
    coef_out, coef_in, totals, coef_ss, coef_rs, total_ss, total_rs, *rest = scratch[2 * N_LAYER_SCRATCH :]
    layers = (fine, coarse)
    place = Place()
    samples = Samples(coarse, place, rest)

    for which in (BANK, UPSTREAM, INPUTS, COEFS):
        for layer in layers:
            load(layer, which).start()
    barrier = pltpu.get_barrier_semaphore()

    def greet(device):
        pl.semaphore_signal(barrier, inc=1, device_id=device, device_id_type=MESH)

    loop(1, N_XY, lambda n: greet(place.at_xy((place.xy + n) % N_XY)))
    for step in (1, N_Z - 1):
        greet(place.at_z((place.z + step) % N_Z))
    loop(1, N_CHAN, lambda n: greet(place.at_chan((place.chan + n) % N_CHAN)))
    for layer in layers:
        arrange_bank(layer, place)
    shift_upstream(fine)
    pl.semaphore_wait(barrier, N_XY + N_CHAN)

    for layer in layers:
        for kind in (0, 1):
            bank_copy(layer, place, kind).start()
    samples.send()
    send_grads(fine, place)
    forward_bank(fine, place)
    for layer in layers:
        spread_coefs(layer, place)
    forward_bank(coarse, place)
    send_kernels(fine, place)
    samples.grads()
    send_parts(coarse, place)
    mix_kernels(coarse, place)
    samples.send_diffs()
    relay_parts(coarse, place)
    coarse_sums = coef_sums(coarse)
    all_grads(fine, place).wait_recv()
    send_parts(fine, place)
    fine_sums = coef_sums(fine)
    shape = (N_XY, 8, GROUP)
    wide_sums = [jnp.broadcast_to(sums[:, None, :], shape) for sums in (fine_sums, coarse_sums)]
    coef_out[...] = jnp.where(iota(shape, 1) == 0, *wide_sums)
    coef_refs = (coef_out, coef_in, coef_ss, coef_rs, place)
    loop(1, N_XY, lambda n: coef_copy(*coef_refs, (place.xy + n) % N_XY).start())
    coef_in[place.xy] = coef_out[place.xy]
    samples.all_copies(2).wait_recv()

    def coarse_diff(chan):
        coarse.diff[...] = samples.diff_in[rows_of(chan, GROUP)].astype(F32)

    relay_parts(fine, place)
    send_diffs(coarse, place, coarse_diff)
    all_coefs(*coef_refs).wait_recv()
    totals[place.chan] = coef_in[...].sum(axis=0)
    total_refs = (totals, total_ss, total_rs, place)
    loop(1, N_CHAN, lambda n: total_copy(*total_refs, (place.chan + n) % N_CHAN, place.chan).start())
    send_diffs(fine, place, functools.partial(diff_of, fine, place))
    finish_update(coarse, place)
    finish_delta(coarse, place)
    loop(1, N_CHAN, lambda n: total_copy(*total_refs, place.chan, (place.chan + n) % N_CHAN).wait_recv())
    total = totals[...].sum(axis=0)
    for index, layer in enumerate(layers):
        finish_logit(layer, place, total[index : index + 1, 0:BANKS])
    finish_update(fine, place)
    finish_delta(fine, place)

    for layer in layers:
        for kind in range(4):
            bank_copy(layer, place, kind).wait_send()
        for kind in range(6):
            part_copy(layer, place, kind).wait_send()
        for kind in range(3):
            diff_copy(layer, place, kind).wait_send()
    all_grads(fine, place).wait_send()
    many_kernels(fine, place, 0, 0, N_XY - 1).wait_send()
    for which in range(3):
        samples.all_copies(which).wait_send()
    all_coefs(*coef_refs).wait_send()
    loop(1, N_CHAN, lambda n: total_copy(*total_refs, (place.chan + n) % N_CHAN, place.chan).wait_send())


def store(*refs):
    given, out, held, (in_sem, out_sem) = refs[:6], refs[6:12], refs[12:18], refs[18:]
    loads = [pltpu.make_async_copy(given[n], held[n], in_sem.at[n]) for n in range(6)]
    stores = [pltpu.make_async_copy(held[n], out[n], out_sem.at[n]) for n in range(6)]
    for copy in loads:
        copy.start()
    for first, second in zip(loads, stores):
        first.wait()
        second.start()
    for copy in stores:
        copy.wait()


def per_device(
    fine_inputs,
    fine_upstream,
    fine_bank,
    fine_coefs,
    coarse_inputs,
    coarse_upstream,
    coarse_bank,
    coarse_coefs,
):
    vmem = pl.BlockSpec(memory_space=pltpu.VMEM)
    hbm = pl.BlockSpec(memory_space=pltpu.HBM)
    out_shape = []
    for side in (FINE_SIDE, COARSE_SIDE):
        out_shape += [
            jax.ShapeDtypeStruct((side * side, GROUP), BF16),
            jax.ShapeDtypeStruct((BANKS, TAPS, OWN, GROUP), F32),
            jax.ShapeDtypeStruct((1, BANKS), F32),
        ]
    results = pl.pallas_call(
        kernel,
        out_shape=out_shape,
        in_specs=[hbm] * 8,
        out_specs=[vmem] * 6,
        scratch_shapes=layer_scratch(FINE_SIDE)
        + layer_scratch(COARSE_SIDE)
        + [
            pltpu.VMEM((N_XY, 8, GROUP), F32),
            pltpu.VMEM((N_XY, 8, GROUP), F32),
            pltpu.VMEM((N_CHAN, 8, GROUP), F32),
            pltpu.SemaphoreType.DMA((1,)),
            pltpu.SemaphoreType.DMA((1,)),
            pltpu.SemaphoreType.DMA((N_CHAN,)),
            pltpu.SemaphoreType.DMA((N_CHAN,)),
            pltpu.VMEM((N_XY, COARSE_SIDE * COARSE_SIDE, GROUP), BF16),
            pltpu.VMEM((CHANNELS, COARSE_SIDE * COARSE_SIDE), BF16),
            pltpu.VMEM((N_XY, COARSE_SIDE * COARSE_SIDE + 2 * COARSE_SIDE, ROW3), BF16),
            pltpu.VMEM((CHANNELS, COARSE_SIDE * COARSE_SIDE), BF16),
            pltpu.VMEM((CHANNELS, COARSE_SIDE * COARSE_SIDE), BF16),
        ]
        + [pltpu.SemaphoreType.DMA((1,))] * 6,
        compiler_params=pltpu.CompilerParams(
            collective_id=0, has_side_effects=True, vmem_limit_bytes=62 * MIB
        ),
    )(
        fine_inputs.reshape(FINE_SIDE * FINE_SIDE, CHANNELS),
        fine_upstream.reshape(FINE_SIDE * FINE_SIDE, GROUP),
        fine_bank,
        fine_coefs.T,
        coarse_inputs.reshape(COARSE_SIDE * COARSE_SIDE, CHANNELS),
        coarse_upstream.reshape(COARSE_SIDE * COARSE_SIDE, GROUP),
        coarse_bank,
        coarse_coefs.T,
    )
    fine_delta, fine_update, fine_logit, coarse_delta, coarse_update, coarse_logit = pl.pallas_call(
        store,
        out_shape=out_shape,
        in_specs=[hbm] * 6,
        out_specs=[hbm] * 6,
        scratch_shapes=[pltpu.VMEM(out.shape, out.dtype) for out in out_shape]
        + [pltpu.SemaphoreType.DMA((6,)), pltpu.SemaphoreType.DMA((6,))],
        compiler_params=pltpu.CompilerParams(vmem_limit_bytes=62 * MIB),
    )(*results)
    return (
        fine_delta.reshape(1, FINE_SIDE, FINE_SIDE, GROUP),
        fine_update,
        fine_logit,
        coarse_delta.reshape(1, COARSE_SIDE, COARSE_SIDE, GROUP),
        coarse_update,
        coarse_logit,
    )


def solution(mesh):
    return jax.shard_map(
        per_device,
        mesh=mesh,
        in_specs=(
            P("batch", None, None, None),
            P("batch", None, None, "chan"),
            P(None, None, "batch", "chan"),
            P(),
            P("batch", None, None, None),
            P("batch", None, None, "chan"),
            P(None, None, "batch", "chan"),
            P(),
        ),
        out_specs=(
            P("batch", None, None, "chan"),
            P(None, None, "batch", "chan"),
            P("batch", None),
            P("batch", None, None, "chan"),
            P(None, None, "batch", "chan"),
            P("batch", None),
        ),
        check_vma=False,
    )
```

```python
import functools

import jax
import jax.numpy as jnp
from jax import lax
from jax.experimental import pallas as pl
from jax.experimental.pallas import tpu as pltpu
from jax.sharding import PartitionSpec as P

BANKS = 8
TAPS = 9
CHANNELS = 512
GROUP = 128
FINE_SIDE = 32
COARSE_SIDE = 16
STEP = 128
AT_ONCE = 4
SAMPLES = 64
N_XY = 16
N_Z = 4
N_CHAN = 4
ROWS = CHANNELS // N_XY
OWN = 8
WIDE = TAPS * GROUP
ROW3 = 3 * GROUP
BLOCK = BANKS * OWN
HALF = BLOCK // 2
BANK_ROWS = N_Z * BLOCK

MIB = 1024 * 1024
MESH = pl.DeviceIdType.MESH
HIGH = lax.Precision.HIGHEST
F32 = jnp.float32
BF16 = jnp.bfloat16


def iota(shape, axis):
    return lax.broadcasted_iota(jnp.int32, shape, axis)


def mm(a, b, contract, precision=None):
    dims = (((contract[0],), (contract[1],)), ((), ()))
    return lax.dot_general(a, b, dims, precision=precision, preferred_element_type=F32)


class Layer:
    def __init__(self, side, args, delta, update, logit, scratch):
        self.side, self.args = side, args
        self.delta, self.update, self.logit = delta, update, logit
        (
            self.inputs, self.upstream, self.bank, self.coefs, self.load_sem,
            self.shifts, self.flipped, self.spread, self.cross, self.banks, self.mix, self.back,
            self.grad_out, self.grad_in, self.kern_out, self.kern_in,
            self.part, self.part_out, self.part_in, self.relay, self.diff, self.diff_out, self.diff_in,
            self.bank_ss, self.bank_rs, self.grad_ss, self.grad_rs, self.kern_ss, self.kern_rs,
            self.part_ss, self.part_rs, self.diff_ss, self.diff_rs,
        ) = scratch


def layer_scratch(side):
    pixels = side * side
    diff = (pixels, GROUP) if side == FINE_SIDE else (GROUP, pixels)
    return [
        pltpu.VMEM((pixels, CHANNELS), BF16),
        pltpu.VMEM((pixels, GROUP), BF16),
        pltpu.VMEM((BANKS, TAPS, OWN, GROUP), BF16),
        pltpu.VMEM((BANKS, SAMPLES), F32),
        pltpu.SemaphoreType.DMA((4,)),
        pltpu.VMEM((pixels + 2 * side, ROW3), BF16),
        pltpu.VMEM((CHANNELS, pixels), BF16),
        pltpu.VMEM((N_XY, BANK_ROWS), F32),
        pltpu.VMEM((N_XY, BANK_ROWS), F32),
        pltpu.VMEM((BANK_ROWS, WIDE), BF16),
        pltpu.VMEM((2, CHANNELS, BANK_ROWS), BF16),
        pltpu.VMEM((2, BANK_ROWS, CHANNELS), BF16),
        pltpu.VMEM((CHANNELS, WIDE), BF16),
        pltpu.VMEM((CHANNELS, WIDE), BF16),
        pltpu.VMEM((CHANNELS, WIDE), BF16),
        pltpu.VMEM((CHANNELS, WIDE), BF16),
        pltpu.VMEM((N_Z, BLOCK, WIDE), F32),
        pltpu.VMEM((N_Z, BLOCK, WIDE), BF16),
        pltpu.VMEM((2, BLOCK, WIDE), BF16),
        pltpu.VMEM((2, HALF, WIDE), BF16),
        pltpu.VMEM(diff, F32),
        pltpu.VMEM((3, *diff), BF16),
        pltpu.VMEM((3, *diff), BF16),
    ] + [
        pltpu.SemaphoreType.DMA((n,))
        for n in (4, 4, 1, 1, 1, 4, 6, 6, 3, 3)
    ]


N_LAYER_SCRATCH = 33


class Place:
    def __init__(self):
        self.batch = lax.axis_index("batch")
        self.chan = lax.axis_index("chan")
        self.xy = self.batch // N_Z
        self.z = self.batch % N_Z
        self.sibling = self.chan + 1 - 2 * (self.chan % 2)
        self.across = (self.chan + 2) % N_CHAN

    def at_xy(self, xy):
        return (xy * N_Z + self.z, self.chan)

    def at_z(self, z):
        return (self.xy * N_Z + z, self.chan)

    def at_chan(self, chan):
        return (self.batch, chan)


def rows_of(index, count):
    return pl.ds(pl.multiple_of(index * count, count), count)


def bank_copy(layer, place, kind, received=False):
    step = N_Z - 1 if kind % 2 else 1
    origin = place.z if kind < 2 else (place.z + N_Z - step) % N_Z
    if received:
        origin = (origin + N_Z - step) % N_Z
    if kind < 2:
        rows = rows_of(origin, BLOCK)
    else:
        rows = rows_of(2 * origin + kind - 2, HALF)
    return pltpu.make_async_remote_copy(
        src_ref=layer.banks.at[rows],
        dst_ref=layer.banks.at[rows],
        send_sem=layer.bank_ss.at[kind],
        recv_sem=layer.bank_rs.at[kind],
        device_id=place.at_z((place.z + step) % N_Z),
        device_id_type=MESH,
    )


def grad_copy(layer, place, xy_to):
    return pltpu.make_async_remote_copy(
        src_ref=layer.grad_out.at[rows_of(xy_to, ROWS)],
        dst_ref=layer.grad_in.at[rows_of(place.xy, ROWS)],
        send_sem=layer.grad_ss.at[0],
        recv_sem=layer.grad_rs.at[0],
        device_id=place.at_xy(xy_to),
        device_id_type=MESH,
    )


def all_grads(layer, place):
    rows = pl.ds(0, (N_XY - 1) * ROWS)
    return pltpu.make_async_remote_copy(
        src_ref=layer.grad_out.at[rows],
        dst_ref=layer.grad_in.at[rows],
        send_sem=layer.grad_ss.at[0],
        recv_sem=layer.grad_rs.at[0],
        device_id=place.at_xy((place.xy + 1) % N_XY),
        device_id_type=MESH,
    )


def kern_copy(layer, place, xy_to):
    return pltpu.make_async_remote_copy(
        src_ref=layer.kern_out.at[rows_of(xy_to, ROWS)],
        dst_ref=layer.kern_in.at[rows_of(place.xy, ROWS)],
        send_sem=layer.kern_ss.at[0],
        recv_sem=layer.kern_rs.at[place.xy // 4],
        device_id=place.at_xy(xy_to),
        device_id_type=MESH,
    )


def many_kernels(layer, place, y, first, blocks):
    rows = pl.ds(pl.multiple_of(first * ROWS, ROWS), blocks * ROWS)
    return pltpu.make_async_remote_copy(
        src_ref=layer.kern_out.at[rows],
        dst_ref=layer.kern_in.at[rows],
        send_sem=layer.kern_ss.at[0],
        recv_sem=layer.kern_rs.at[y],
        device_id=place.at_xy((place.xy + 1) % N_XY),
        device_id_type=MESH,
    )


def part_copy(layer, place, kind):
    to = (place.z + (1 if kind in (0, 2, 3) else N_Z - 1)) % N_Z
    target = (place.z + 2) % N_Z if kind < 2 else to
    half = (0, 1, 1, 0, 0, 1)[kind]
    rows = pl.ds(half * HALF, HALF)
    if kind < 2:
        landing = layer.relay.at[kind]
    else:
        landing = layer.part_in.at[0 if kind < 4 else 1, rows]
    return pltpu.make_async_remote_copy(
        src_ref=layer.part_out.at[target, rows],
        dst_ref=landing,
        send_sem=layer.part_ss.at[kind],
        recv_sem=layer.part_rs.at[kind],
        device_id=place.at_z(to),
        device_id_type=MESH,
    )


def diff_copy(layer, place, kind):
    return pltpu.make_async_remote_copy(
        src_ref=layer.diff_out.at[kind],
        dst_ref=layer.diff_in.at[kind],
        send_sem=layer.diff_ss.at[kind],
        recv_sem=layer.diff_rs.at[kind],
        device_id=place.at_chan(place.across if kind == 1 else place.sibling),
        device_id_type=MESH,
    )


def coef_copy(out_ref, in_ref, send_sem, recv_sem, place, xy_to):
    return pltpu.make_async_remote_copy(
        src_ref=out_ref.at[xy_to],
        dst_ref=in_ref.at[place.xy],
        send_sem=send_sem.at[0],
        recv_sem=recv_sem.at[0],
        device_id=place.at_xy(xy_to),
        device_id_type=MESH,
    )


def all_coefs(out_ref, in_ref, send_sem, recv_sem, place):
    return pltpu.make_async_remote_copy(
        src_ref=out_ref.at[0 : N_XY - 1],
        dst_ref=in_ref.at[0 : N_XY - 1],
        send_sem=send_sem.at[0],
        recv_sem=recv_sem.at[0],
        device_id=place.at_xy((place.xy + 1) % N_XY),
        device_id_type=MESH,
    )


def total_copy(ref, send_sem, recv_sem, place, chan_to, chan_from):
    return pltpu.make_async_remote_copy(
        src_ref=ref.at[chan_from],
        dst_ref=ref.at[chan_from],
        send_sem=send_sem.at[chan_to],
        recv_sem=recv_sem.at[chan_from],
        device_id=place.at_chan(chan_to),
        device_id_type=MESH,
    )


def loop(low, high, body):
    lax.fori_loop(low, high, lambda n, carry: (body(n), carry)[1], 0)


INPUTS, UPSTREAM, BANK, COEFS = range(4)


def load(layer, which):
    held = (layer.inputs, layer.upstream, layer.bank, layer.coefs)[which]
    return pltpu.make_async_copy(layer.args[which], held, layer.load_sem.at[which])


def arrange_bank(layer, place):
    load(layer, BANK).wait()

    def move(tap):
        rows = layer.bank[:, tap].astype(F32).reshape(BLOCK, GROUP).astype(BF16)
        layer.banks[rows_of(place.z, BLOCK), rows_of(tap, GROUP)] = rows

    loop(0, TAPS, move)


def clear_edges(shifts, side):
    zeros = jnp.zeros((side, ROW3), BF16)
    shifts[0:side] = zeros
    shifts[shifts.shape[0] - side : shifts.shape[0]] = zeros


def shift_rows(upstream, shifts, side, n):
    column = iota((STEP, GROUP), 0) & (side - 1)
    up = upstream[rows_of(n, STEP)].astype(F32)
    after = jnp.where(column < side - 1, pltpu.roll(up, STEP - 1, 0), 0.0)
    before = jnp.where(column > 0, pltpu.roll(up, 1, 0), 0.0)
    rows = pl.ds(pl.multiple_of(n * STEP + side, side), STEP)
    for index, value in enumerate((after, up, before)):
        shifts[rows, index * GROUP : (index + 1) * GROUP] = value.astype(BF16)


def shift_upstream(layer):
    load(layer, UPSTREAM).wait()
    clear_edges(layer.shifts, layer.side)
    loop(0, layer.side * layer.side // STEP, lambda n: shift_rows(layer.upstream, layer.shifts, layer.side, n))


def window(layer, row_shift, first, count):
    start = pl.multiple_of((2 - row_shift) * layer.side + first, layer.side)
    return layer.shifts[pl.ds(start, count)]


def split(value, ref, rows):
    hi = value.astype(BF16)
    ref[0, rows] = hi
    ref[1, rows] = (value - hi.astype(F32)).astype(BF16)


def spread_coefs(layer, place):
    load(layer, COEFS).wait()
    chosen = iota((SAMPLES, N_XY), 0) == iota((SAMPLES, N_XY), 1) * N_Z + place.z
    own = mm(layer.coefs[...], chosen.astype(F32), (1, 0), HIGH)
    col = iota((BANKS, BANK_ROWS), 1)
    wide = ((col // OWN) % BANKS == iota((BANKS, BANK_ROWS), 0)).astype(F32)
    layer.spread[...] = mm(own, wide, (0, 0), HIGH)
    same = diagonal(ROWS)

    def sample(n):
        row = jnp.broadcast_to(layer.spread[pl.ds(n, 1), :], (ROWS, BANK_ROWS))
        split(jnp.where(same, row, 0.0), layer.mix, rows_of(n, ROWS))

    loop(0, N_XY, sample)
    col = iota((N_XY, CHANNELS), 1)
    tall = mm(own, (col // ROWS == iota((N_XY, CHANNELS), 0)).astype(F32), (1, 0), HIGH)
    tall = jnp.broadcast_to(tall[:, None, :], (BANKS, OWN, CHANNELS)).reshape(BLOCK, CHANNELS)
    row, col = iota((BLOCK, CHANNELS), 0), iota((BLOCK, CHANNELS), 1)

    def block(n):
        same = n * OWN + row % OWN == col % ROWS
        split(jnp.where(same, tall, 0.0), layer.back, rows_of(n, BLOCK))

    loop(0, N_Z, block)


def diagonal(rows):
    shape = (rows, BANK_ROWS)
    row, col = iota(shape, 0), iota(shape, 1)
    return row % ROWS == (col // BLOCK) * OWN + col % OWN


AROUND = (
    (1, 0), (0, 1), (3, 0), (0, 3), (1, 1), (3, 3), (2, 0), (0, 2),
    (1, 3), (3, 1), (2, 1), (2, 3), (1, 2), (3, 2), (2, 2),
)


def send_rows(place, copy):
    y, x = place.xy // 4, place.xy % 4
    for step_x, step_y in AROUND:
        copy((y + step_y) % 4 * 4 + (x + step_x) % 4).start()


def flip_inputs(layer):
    load(layer, INPUTS).wait()

    def flip(n):
        layer.flipped[rows_of(n, GROUP)] = layer.inputs[:, rows_of(n, GROUP)].T

    loop(0, CHANNELS // GROUP, flip)


def send_grads(layer, place):
    flip_inputs(layer)
    pixels = layer.side * layer.side

    def chunk(n):
        row_shift, part = n // 2, rows_of(n % 2, 2 * GROUP)
        grad = mm(layer.flipped[part], window(layer, row_shift, 0, pixels), (1, 0)) * (1.0 / layer.side)
        layer.grad_out[part, rows_of(row_shift, ROW3)] = grad.astype(BF16)

    loop(0, 6, chunk)
    send_rows(place, functools.partial(grad_copy, layer, place))
    own = rows_of(place.xy, ROWS)
    layer.grad_in[own, :] = layer.grad_out[own, :]


def forward_bank(layer, place):
    for kind in (0, 1):
        bank_copy(layer, place, kind, received=True).wait_recv()
        bank_copy(layer, place, kind + 2).start()


def mix_kernels(layer, place):
    for kind in (2, 3):
        bank_copy(layer, place, kind, received=True).wait_recv()

    def chunk(n):
        cols, part = rows_of(n // 2, ROW3), rows_of(n % 2, 2 * GROUP)
        banks = layer.banks[:, cols]
        mixed = mm(layer.mix[0, part], banks, (1, 0)) + mm(layer.mix[1, part], banks, (1, 0))
        layer.kern_out[part, cols] = mixed.astype(BF16)

    loop(0, 6, chunk)


def send_kernels(layer, place):
    mix_kernels(layer, place)
    send_rows(place, functools.partial(kern_copy, layer, place))
    own = rows_of(place.xy, ROWS)
    layer.kern_in[own, :] = layer.kern_out[own, :]


class Samples:
    def __init__(self, layer, place, scratch):
        self.layer, self.place = layer, place
        (
            self.upstream, self.inputs, self.shifts, self.diff_out, self.diff_in,
            self.up_ss, self.up_rs, self.in_ss, self.in_rs, self.diff_ss, self.diff_rs,
        ) = scratch

    def copy(self, source, target, send_sem, recv_sem, to):
        return pltpu.make_async_remote_copy(
            src_ref=source,
            dst_ref=target,
            send_sem=send_sem.at[0],
            recv_sem=recv_sem.at[0],
            device_id=self.place.at_xy(to),
            device_id_type=MESH,
        )

    def up_copy(self, to):
        return self.copy(self.layer.upstream, self.upstream.at[self.place.xy], self.up_ss, self.up_rs, to)

    def in_copy(self, to):
        rows, here = rows_of(to, ROWS), rows_of(self.place.xy, ROWS)
        return self.copy(self.layer.flipped.at[rows], self.inputs.at[here], self.in_ss, self.in_rs, to)

    def diff_copy(self, to):
        rows, here = rows_of(to, ROWS), rows_of(self.place.xy, ROWS)
        return self.copy(self.diff_out.at[rows], self.diff_in.at[here], self.diff_ss, self.diff_rs, to)

    def all_copies(self, which):
        some, rows = pl.ds(0, N_XY - 1), pl.ds(0, (N_XY - 1) * ROWS)
        refs = (
            (self.upstream.at[some], self.upstream.at[some], self.up_ss, self.up_rs),
            (self.layer.flipped.at[rows], self.inputs.at[rows], self.in_ss, self.in_rs),
            (self.diff_out.at[rows], self.diff_in.at[rows], self.diff_ss, self.diff_rs),
        )[which]
        return self.copy(*refs, (self.place.xy + 1) % N_XY)

    def send(self):
        place, own = self.place, rows_of(self.place.xy, ROWS)
        load(self.layer, UPSTREAM).wait()
        send_rows(place, self.up_copy)
        flip_inputs(self.layer)
        send_rows(place, self.in_copy)
        self.upstream[place.xy] = self.layer.upstream[...]
        self.inputs[own] = self.layer.flipped[own]

    def window(self, sample, row_shift):
        side = self.layer.side
        start = (2 - row_shift) * side
        return self.shifts[sample, start : start + side * side]

    def grads(self):
        layer, side = self.layer, self.layer.side
        self.all_copies(0).wait_recv()
        self.all_copies(1).wait_recv()

        def some(n):
            picked = [n * AT_ONCE + at for at in range(AT_ONCE)]
            for sample in picked:
                clear_edges(self.shifts.at[sample], side)
                for part in range(side * side // STEP):
                    shift_rows(self.upstream.at[sample], self.shifts.at[sample], side, part)
            for sample in picked:
                rows = rows_of(sample, ROWS)
                for row_shift in range(3):
                    grad = mm(self.inputs[rows], self.window(sample, row_shift), (1, 0)) * (1.0 / side)
                    layer.grad_in[rows, row_shift * ROW3 : (row_shift + 1) * ROW3] = grad.astype(BF16)

        loop(0, N_XY // AT_ONCE, some)

    def send_diffs(self):
        def some(n):
            for at in range(AT_ONCE):
                sample = n * AT_ONCE + at
                rows, diff = rows_of(sample, ROWS), None
                for row_shift in range(3):
                    cols = slice(row_shift * ROW3, (row_shift + 1) * ROW3)
                    term = mm(self.layer.kern_out[rows, cols], self.window(sample, row_shift), (1, 1))
                    diff = term if diff is None else diff + term
                self.diff_out[rows] = diff.astype(BF16)

        loop(0, N_XY // AT_ONCE, some)
        send_rows(self.place, self.diff_copy)
        own = rows_of(self.place.xy, ROWS)
        self.diff_in[own] = self.diff_out[own]


def send_parts(layer, place):
    def some(n):
        cols = rows_of(n, ROW3)
        grads = layer.grad_in[:, cols]
        total = mm(layer.back[0], grads, (1, 0)) + mm(layer.back[1], grads, (1, 0))
        total = total.reshape(N_Z, BLOCK, ROW3)
        layer.part[:, :, cols] = total
        layer.part_out[:, :, cols] = total.astype(BF16)

    loop(0, 3, some)
    for kind in (0, 1, 2, 4):
        part_copy(layer, place, kind).start()


def relay_parts(layer, place):
    for kind, half in ((0, 0), (1, 1)):
        part_copy(layer, place, kind).wait_recv()
        target = (place.z + (1 if kind == 0 else N_Z - 1)) % N_Z
        rows = slice(half * HALF, (half + 1) * HALF)
        total = layer.part[target, rows] + layer.relay[kind].astype(F32)
        layer.part_out[target, rows] = total.astype(BF16)
        part_copy(layer, place, 3 if kind == 0 else 5).start()


def coef_sums(layer):
    same = diagonal(STEP)

    def some(n):
        cross = mm(layer.grad_in[rows_of(n, STEP)], layer.banks[...], (1, 1))
        cross = jnp.where(same, cross, 0.0).reshape(STEP // ROWS, ROWS, BANK_ROWS).sum(axis=1)
        for sample in range(STEP // ROWS):
            layer.cross[pl.ds(n * (STEP // ROWS) + sample, 1), :] = cross[sample : sample + 1]

    loop(0, CHANNELS // STEP, some)
    row = iota((BANK_ROWS, GROUP), 0)
    pick = ((row // OWN) % BANKS == iota((BANK_ROWS, GROUP), 1)).astype(F32)
    return mm(layer.cross[...], pick, (1, 0), HIGH)


def diff_of(layer, place, chan):
    y, my_y = chan, place.xy // 4

    @pl.when(y != my_y)
    def _():
        many_kernels(layer, place, y, y * 4, 4).wait_recv()

    @pl.when(y == my_y)
    def _():
        many_kernels(layer, place, y, y * 4, 3).wait_recv()

    part, size = rows_of(chan, GROUP), 2 * STEP

    def some(n):
        diff = mm(window(layer, 0, n * size, size), layer.kern_in[part, 0:ROW3], (1, 1))
        for row_shift in (1, 2):
            cols = slice(row_shift * ROW3, (row_shift + 1) * ROW3)
            diff = diff + mm(window(layer, row_shift, n * size, size), layer.kern_in[part, cols], (1, 1))
        layer.diff[rows_of(n, size)] = diff

    loop(0, layer.side * layer.side // size, some)


def send_diffs(layer, place, diff_of):
    def target(n):
        base = (place.chan + 2 * (1 - n // 2)) % N_CHAN
        diff_of(base + (1 - n % 2) * (1 - 2 * (place.chan % 2)))

        @pl.when(n == 0)
        def _():
            layer.diff_out[0] = layer.diff[...].astype(BF16)
            diff_copy(layer, place, 0).start()

        @pl.when(n == 1)
        def _():
            diff_copy(layer, place, 0).wait_recv()
            layer.diff_out[1] = (layer.diff[...] + layer.diff_in[0].astype(F32)).astype(BF16)
            diff_copy(layer, place, 1).start()

        @pl.when(n == 2)
        def _():
            layer.diff_out[2] = layer.diff[...].astype(BF16)
            diff_copy(layer, place, 2).start()

    loop(0, N_CHAN, target)


def finish_update(layer, place):
    for kind in (2, 3, 4, 5):
        part_copy(layer, place, kind).wait_recv()
    total = layer.part[place.z] + layer.part_in[0].astype(F32) + layer.part_in[1].astype(F32)
    for tap in range(TAPS):
        cols = total[:, tap * GROUP : (tap + 1) * GROUP]
        layer.update[:, tap] = cols.reshape(BANKS, OWN, GROUP)


def finish_delta(layer, place):
    total = layer.diff[...]
    for kind in (2, 1):
        diff_copy(layer, place, kind).wait_recv()
        total = total + layer.diff_in[kind].astype(F32)
    layer.delta[...] = (total if layer.side == FINE_SIDE else total.T).astype(BF16)


def finish_logit(layer, place, total):
    chosen = (iota((1, SAMPLES), 1) == place.batch).astype(F32)
    coefs = mm(chosen, layer.coefs[...], (1, 1), HIGH)
    layer.logit[...] = coefs * (total - jnp.sum(coefs * total, axis=1, keepdims=True))


def kernel(*refs):
    args, outs, scratch = refs[:8], refs[8:14], refs[14:]
    fine = Layer(FINE_SIDE, args[:4], *outs[:3], scratch[:N_LAYER_SCRATCH])
    coarse = Layer(COARSE_SIDE, args[4:], *outs[3:], scratch[N_LAYER_SCRATCH : 2 * N_LAYER_SCRATCH])
    coef_out, coef_in, totals, coef_ss, coef_rs, total_ss, total_rs, *rest = scratch[2 * N_LAYER_SCRATCH :]
    layers = (fine, coarse)
    place = Place()
    samples = Samples(coarse, place, rest)

    for which in (BANK, UPSTREAM, INPUTS, COEFS):
        for layer in layers:
            load(layer, which).start()
    barrier = pltpu.get_barrier_semaphore()

    def greet(device):
        pl.semaphore_signal(barrier, inc=1, device_id=device, device_id_type=MESH)

    loop(1, N_XY, lambda n: greet(place.at_xy((place.xy + n) % N_XY)))
    for step in (1, N_Z - 1):
        greet(place.at_z((place.z + step) % N_Z))
    loop(1, N_CHAN, lambda n: greet(place.at_chan((place.chan + n) % N_CHAN)))
    for layer in layers:
        arrange_bank(layer, place)
    shift_upstream(fine)
    pl.semaphore_wait(barrier, N_XY + N_CHAN)

    for layer in layers:
        for kind in (0, 1):
            bank_copy(layer, place, kind).start()
    samples.send()
    send_grads(fine, place)
    forward_bank(fine, place)
    for layer in layers:
        spread_coefs(layer, place)
    forward_bank(coarse, place)
    send_kernels(fine, place)
    samples.grads()
    send_parts(coarse, place)
    mix_kernels(coarse, place)
    samples.send_diffs()
    relay_parts(coarse, place)
    coarse_sums = coef_sums(coarse)
    all_grads(fine, place).wait_recv()
    send_parts(fine, place)
    fine_sums = coef_sums(fine)
    relay_parts(fine, place)
    shape = (N_XY, 8, GROUP)
    wide_sums = [jnp.broadcast_to(sums[:, None, :], shape) for sums in (fine_sums, coarse_sums)]
    coef_out[...] = jnp.where(iota(shape, 1) == 0, *wide_sums)
    coef_refs = (coef_out, coef_in, coef_ss, coef_rs, place)
    loop(1, N_XY, lambda n: coef_copy(*coef_refs, (place.xy + n) % N_XY).start())
    coef_in[place.xy] = coef_out[place.xy]
    samples.all_copies(2).wait_recv()

    def coarse_diff(chan):
        coarse.diff[...] = samples.diff_in[rows_of(chan, GROUP)].astype(F32)

    send_diffs(coarse, place, coarse_diff)
    all_coefs(*coef_refs).wait_recv()
    totals[place.chan] = coef_in[...].sum(axis=0)
    total_refs = (totals, total_ss, total_rs, place)
    loop(1, N_CHAN, lambda n: total_copy(*total_refs, (place.chan + n) % N_CHAN, place.chan).start())
    send_diffs(fine, place, functools.partial(diff_of, fine, place))
    finish_update(coarse, place)
    finish_delta(coarse, place)
    loop(1, N_CHAN, lambda n: total_copy(*total_refs, place.chan, (place.chan + n) % N_CHAN).wait_recv())
    total = totals[...].sum(axis=0)
    for index, layer in enumerate(layers):
        finish_logit(layer, place, total[index : index + 1, 0:BANKS])
    finish_update(fine, place)
    finish_delta(fine, place)

    for layer in layers:
        for kind in range(4):
            bank_copy(layer, place, kind).wait_send()
        for kind in range(6):
            part_copy(layer, place, kind).wait_send()
        for kind in range(3):
            diff_copy(layer, place, kind).wait_send()
    all_grads(fine, place).wait_send()
    many_kernels(fine, place, 0, 0, N_XY - 1).wait_send()
    for which in range(3):
        samples.all_copies(which).wait_send()
    all_coefs(*coef_refs).wait_send()
    loop(1, N_CHAN, lambda n: total_copy(*total_refs, (place.chan + n) % N_CHAN, place.chan).wait_send())


def store(*refs):
    given, out, held, (in_sem, out_sem) = refs[:6], refs[6:12], refs[12:18], refs[18:]
    loads = [pltpu.make_async_copy(given[n], held[n], in_sem.at[n]) for n in range(6)]
    stores = [pltpu.make_async_copy(held[n], out[n], out_sem.at[n]) for n in range(6)]
    for copy in loads:
        copy.start()
    for first, second in zip(loads, stores):
        first.wait()
        second.start()
    for copy in stores:
        copy.wait()


def per_device(
    fine_inputs,
    fine_upstream,
    fine_bank,
    fine_coefs,
    coarse_inputs,
    coarse_upstream,
    coarse_bank,
    coarse_coefs,
):
    vmem = pl.BlockSpec(memory_space=pltpu.VMEM)
    hbm = pl.BlockSpec(memory_space=pltpu.HBM)
    out_shape = []
    for side in (FINE_SIDE, COARSE_SIDE):
        out_shape += [
            jax.ShapeDtypeStruct((side * side, GROUP), BF16),
            jax.ShapeDtypeStruct((BANKS, TAPS, OWN, GROUP), F32),
            jax.ShapeDtypeStruct((1, BANKS), F32),
        ]
    results = pl.pallas_call(
        kernel,
        out_shape=out_shape,
        in_specs=[hbm] * 8,
        out_specs=[vmem] * 6,
        scratch_shapes=layer_scratch(FINE_SIDE)
        + layer_scratch(COARSE_SIDE)
        + [
            pltpu.VMEM((N_XY, 8, GROUP), F32),
            pltpu.VMEM((N_XY, 8, GROUP), F32),
            pltpu.VMEM((N_CHAN, 8, GROUP), F32),
            pltpu.SemaphoreType.DMA((1,)),
            pltpu.SemaphoreType.DMA((1,)),
            pltpu.SemaphoreType.DMA((N_CHAN,)),
            pltpu.SemaphoreType.DMA((N_CHAN,)),
            pltpu.VMEM((N_XY, COARSE_SIDE * COARSE_SIDE, GROUP), BF16),
            pltpu.VMEM((CHANNELS, COARSE_SIDE * COARSE_SIDE), BF16),
            pltpu.VMEM((N_XY, COARSE_SIDE * COARSE_SIDE + 2 * COARSE_SIDE, ROW3), BF16),
            pltpu.VMEM((CHANNELS, COARSE_SIDE * COARSE_SIDE), BF16),
            pltpu.VMEM((CHANNELS, COARSE_SIDE * COARSE_SIDE), BF16),
        ]
        + [pltpu.SemaphoreType.DMA((1,))] * 6,
        compiler_params=pltpu.CompilerParams(
            collective_id=0, has_side_effects=True, vmem_limit_bytes=62 * MIB
        ),
    )(
        fine_inputs.reshape(FINE_SIDE * FINE_SIDE, CHANNELS),
        fine_upstream.reshape(FINE_SIDE * FINE_SIDE, GROUP),
        fine_bank,
        fine_coefs.T,
        coarse_inputs.reshape(COARSE_SIDE * COARSE_SIDE, CHANNELS),
        coarse_upstream.reshape(COARSE_SIDE * COARSE_SIDE, GROUP),
        coarse_bank,
        coarse_coefs.T,
    )
    fine_delta, fine_update, fine_logit, coarse_delta, coarse_update, coarse_logit = pl.pallas_call(
        store,
        out_shape=out_shape,
        in_specs=[hbm] * 6,
        out_specs=[hbm] * 6,
        scratch_shapes=[pltpu.VMEM(out.shape, out.dtype) for out in out_shape]
        + [pltpu.SemaphoreType.DMA((6,)), pltpu.SemaphoreType.DMA((6,))],
        compiler_params=pltpu.CompilerParams(vmem_limit_bytes=62 * MIB),
    )(*results)
    return (
        fine_delta.reshape(1, FINE_SIDE, FINE_SIDE, GROUP),
        fine_update,
        fine_logit,
        coarse_delta.reshape(1, COARSE_SIDE, COARSE_SIDE, GROUP),
        coarse_update,
        coarse_logit,
    )


def solution(mesh):
    return jax.shard_map(
        per_device,
        mesh=mesh,
        in_specs=(
            P("batch", None, None, None),
            P("batch", None, None, "chan"),
            P(None, None, "batch", "chan"),
            P(),
            P("batch", None, None, None),
            P("batch", None, None, "chan"),
            P(None, None, "batch", "chan"),
            P(),
        ),
        out_specs=(
            P("batch", None, None, "chan"),
            P(None, None, "batch", "chan"),
            P("batch", None),
            P("batch", None, None, "chan"),
            P(None, None, "batch", "chan"),
            P("batch", None),
        ),
        check_vma=False,
    )
```
